512 devices in a mesh: tok: 32 (over z, core), wid: 16 (over y, x).
Axes of the slice: x: 4, y: 4, z: 16, core: 2. Of those that a mesh axis runs over, the one named last changes fastest.
Arguments:
- hidden: bfloat16 [16896, 1280], P('tok', 'wid'), may hold values from -30 to 30
- w_qkv: bfloat16 [1280, 1920], P('tok', 'wid'), may hold values from -0.15625 to 0.15625
- w_out: bfloat16 [1280, 1280], P('tok', 'wid'), may hold values from -0.15625 to 0.15625
- w_gate: bfloat16 [1280, 3584], P('tok', 'wid'), may hold values from -0.15625 to 0.15625
- w_up: bfloat16 [1280, 3584], P('tok', 'wid'), may hold values from -0.15625 to 0.15625
- w_down: bfloat16 [3584, 1280], P('wid', 'tok'), may hold values from -0.1875 to 0.1875
- g_attn: float32 [1280], replicated, may hold values from 0.1 to 1.9
- g_ffn: float32 [1280], replicated, may hold values from 0.1 to 1.9
- lengths: int32 [544], P('tok'), may hold values from 0 to 2048, as said below
- k_cache: bfloat16 [544, 2048, 320], P('tok', 'wid'), may hold values from -45 to 45
- v_cache: bfloat16 [544, 2048, 320], P('tok', 'wid'), may hold values from -4 to 4
Outputs:
- output: bfloat16 [16896, 1280], P('tok', 'wid')
- new_kv: bfloat16 [16896, 640], P('tok', 'wid')
The draws below stay inside these ranges and needn't reach their ends.
Inputs may be any that keep to these rules, and one draw needn't show every extreme that they name: `lengths`: each request's entry is at most 2048, and some request has exactly 2048.
All inputs are finite; a program needn't handle non-finite values.
Results may differ from the reference program's by a relative error of at most 0.017.
Values may be sent and summed in bfloat16 or wider, within the bound.
No kernel may reach another device: no remote copies, remote signals or barrier semaphores. Data moves between devices by JAX's collectives and lax.ppermute only.
A program may use at most 64 MiB of HBM per device.

```python
import jax
import jax.numpy as jnp
from jax import lax

D = 1280
HEADS = 20
KV_HEADS = 5
HEAD_DIM = 64
FF = 3584
STRETCH = 512
MAXLEN = 2048
ROWS_T = 528
REQ_T = 17
ROWS = 16896
REQS = 544
QKVW = 1920
KVW = 320
N_TOK = 32


def draw_hidden(key, part):
    first, second, third = jax.random.split(jax.random.fold_in(key, 11), 3)
    base = jnp.clip(jax.random.normal(first, (ROWS, D), jnp.float32), -4.0, 4.0)
    row_scale = jnp.exp(jax.random.uniform(second, (ROWS, 1), jnp.float32, -1.15, 1.15))
    column_scale = jnp.exp(jax.random.uniform(third, (1, D), jnp.float32, -0.7, 0.7))
    return (base * row_scale * column_scale).astype(jnp.bfloat16)


def draw_lengths(key, part):
    first, second, third = jax.random.split(jax.random.fold_in(key, 23), 3)
    one_draw = jax.random.randint(first, (REQS,), 0, MAXLEN + 1)
    other_draw = jax.random.randint(second, (REQS,), 0, MAXLEN + 1)
    chosen = jax.random.randint(third, (), 0, REQS)
    return jnp.minimum(one_draw, other_draw).at[chosen].set(MAXLEN).astype(jnp.int32)


def draw_k_cache(key, part):
    first = jax.random.fold_in(jax.random.fold_in(key, 37), 0)
    base = jnp.clip(jax.random.normal(first, (REQS, MAXLEN, KVW), jnp.float32), -4.0, 4.0)
    return base.astype(jnp.bfloat16)


def raised(drawn, stream_key, source, target, shards_of, factor):
    def block_of(axis_at):
        return (jnp.arange(drawn.shape[axis_at]) // (drawn.shape[axis_at] // shards_of)).reshape((-1,) + (1,) * (drawn.ndim - 1 - axis_at))

    near = jax.random.permutation(stream_key, shards_of)[block_of(target)]
    other_side = (block_of(target) + shards_of // 2) % shards_of
    return jnp.where((block_of(source) == near) | (block_of(source) == other_side), factor * drawn, drawn)


def shard_levels(own_key, shape, pieces, least, high):
    def one(dim, blocks):
        draws = jax.random.uniform(jax.random.fold_in(jax.random.fold_in(own_key, 6), dim), (blocks,), jnp.float32, least / len(pieces), high / len(pieces))
        return jnp.repeat(jnp.exp(draws), shape[dim] // blocks).reshape((-1,) + (1,) * (len(shape) - dim - 1))

    level = one(*pieces[0])
    for cut in pieces[1:]:
        level = level * one(*cut)
    return level


def normal_values(key, extent, scale, bound, pieces=(), kind=jnp.bfloat16):
    entries = scale * jax.random.normal(key, extent, jnp.float32)
    if pieces:
        entries = entries * shard_levels(key, extent, pieces, -0.22, 0.18)
    return jnp.clip(entries, -bound, bound).astype(kind)


def gaussian_with(rng, extent, spread, most, cuts, heavy, kind=jnp.bfloat16):
    values = spread * jax.random.normal(rng, extent, jnp.float32)
    if cuts:
        values = values * shard_levels(rng, extent, cuts, -0.22, 0.18)
    return jnp.clip(raised(values, jax.random.fold_in(rng, 3), *heavy), -most, most).astype(kind)


def setup_inputs(seed: int = 0) -> dict:
    seeds = jax.random.split(jax.random.key(seed), 12)
    return {
        "hidden": draw_hidden(jax.random.fold_in(seeds[11], 71), 0),
        "w_qkv": normal_values(seeds[1], (D, QKVW), D ** -0.5, 0.15625, ((0, 32), (1, 16))),
        "w_out": normal_values(seeds[2], (HEADS * HEAD_DIM, D), (HEADS * HEAD_DIM) ** -0.5, 0.15625, ((0, 32), (1, 16))),
        "w_gate": normal_values(seeds[3], (D, FF), D ** -0.5, 0.15625, ((0, 32), (1, 16))),
        "w_up": normal_values(seeds[4], (D, FF), D ** -0.5, 0.15625, ((0, 32), (1, 16))),
        "w_down": gaussian_with(seeds[5], (FF, D), FF ** -0.5, 0.1875, ((0, 16), (1, 32)), (0, 1, 32, 2.75)),
        "g_attn": jnp.clip(1.0 + 0.18 * jax.random.normal(seeds[6], (D,), jnp.float32), 0.1, 1.9),
        "g_ffn": jnp.clip(1.0 + 0.18 * jax.random.normal(seeds[7], (D,), jnp.float32), 0.1, 1.9),
        "lengths": draw_lengths(jax.random.fold_in(seeds[11], 71), 0),
        "k_cache": draw_k_cache(jax.random.fold_in(seeds[11], 71), 0),
        "v_cache": normal_values(seeds[10], (REQS, MAXLEN, KVW), 1.0, 4.0, ((0, 32), (1, 16))),
    }


EPSILON = 1e-05
MASKED = -1e+30
SCORE_SCALE = 0.125

def settle(values):
    return lax.optimization_barrier(values.astype(jnp.bfloat16))

def norm_rows(values, gain):
    wide = values.astype(jnp.float32)
    mean_square = lax.optimization_barrier(jnp.mean(wide * wide, axis=-1, keepdims=True))
    return (wide * lax.rsqrt(mean_square + EPSILON) * gain).astype(jnp.bfloat16)

def rotate(parts, places):
    half = parts.shape[-1] // 2
    ladder = jnp.arange(half).astype(jnp.float32) * (2.0 / parts.shape[-1])
    freqs = jnp.power(10000.0, -ladder)
    angles = places.astype(jnp.float32)[:, None] * freqs[None, :]
    cosine = jnp.cos(angles)[:, None, :]
    sine = jnp.sin(angles)[:, None, :]
    first = parts[..., :half]
    second = parts[..., half:]
    return jnp.concatenate([first * cosine - second * sine, second * cosine + first * sine], axis=-1)

def positions(owned):
    stretch_rows = owned[0] + jnp.arange(STRETCH).astype(jnp.int32)
    return jnp.concatenate([stretch_rows, owned[1:]])

def attend(inputs):
    query, keys, values, k_old, v_old, owned = inputs
    groups = HEADS // KV_HEADS
    query_heads = query.reshape(ROWS_T, KV_HEADS, groups, HEAD_DIM).astype(jnp.float32)
    old_keys = k_old.reshape(REQ_T, MAXLEN, KV_HEADS, HEAD_DIM).astype(jnp.float32)
    old_values = v_old.reshape(REQ_T, MAXLEN, KV_HEADS, HEAD_DIM).astype(jnp.float32)
    spots = jnp.arange(MAXLEN).astype(jnp.int32)
    live = spots[None, :] < owned[:, None]
    score_stretch = jnp.einsum('rkgd,pkd->rkgp', query_heads[:STRETCH], old_keys[0]) * SCORE_SCALE
    score_stretch = jnp.where(live[0][None, None, None, :], score_stretch, MASKED)
    score_decode = jnp.einsum('jkgd,jpkd->jkgp', query_heads[STRETCH:], old_keys[1:]) * SCORE_SCALE
    score_decode = jnp.where(live[1:][:, None, None, :], score_decode, MASKED)
    row_ids = jnp.arange(ROWS_T).astype(jnp.int32)
    later = row_ids[:, None]
    earlier = row_ids[None, :]
    fresh_ok = (later < STRETCH) & (earlier < STRETCH) & (earlier <= later) | (later >= STRETCH) & (earlier == later)
    score_fresh = jnp.einsum('rkgd,jkd->rkgj', query_heads, keys.astype(jnp.float32)) * SCORE_SCALE
    score_fresh = jnp.where(fresh_ok[:, None, None, :], score_fresh, MASKED)
    peak = jnp.maximum(jnp.concatenate([score_stretch.max(-1), score_decode.max(-1)], axis=0), score_fresh.max(-1))
    expo_stretch = jnp.exp(score_stretch - peak[:STRETCH, :, :, None])
    expo_decode = jnp.exp(score_decode - peak[STRETCH:, :, :, None])
    expo_fresh = jnp.exp(score_fresh - peak[:, :, :, None])
    totals = jnp.concatenate([expo_stretch.sum(-1), expo_decode.sum(-1)], axis=0) + expo_fresh.sum(-1)
    cached = jnp.concatenate([jnp.einsum('rkgp,pkd->rkgd', settle(expo_stretch).astype(jnp.float32), old_values[0]), jnp.einsum('jkgp,jpkd->jkgd', settle(expo_decode).astype(jnp.float32), old_values[1:])], axis=0)
    fresh = jnp.einsum('rkgj,jkd->rkgd', settle(expo_fresh).astype(jnp.float32), values.astype(jnp.float32))
    result = (cached + fresh) / totals[:, :, :, None]
    return result.astype(jnp.bfloat16).reshape(ROWS_T, HEADS * HEAD_DIM)

def reference(hidden, w_qkv, w_out, w_gate, w_up, w_down, g_attn, g_ffn, lengths, k_cache, v_cache):
    query_width = HEADS * HEAD_DIM
    normed = norm_rows(hidden, g_attn)
    mixed = settle(jnp.dot(normed, w_qkv, preferred_element_type=jnp.float32))
    owned = lengths.reshape(N_TOK, REQ_T)
    places = jax.vmap(positions)(owned).reshape(ROWS)
    query = rotate(mixed[:, :query_width].astype(jnp.float32).reshape(ROWS, HEADS, HEAD_DIM), places).astype(jnp.bfloat16)
    keys = rotate(mixed[:, query_width:query_width + KVW].astype(jnp.float32).reshape(ROWS, KV_HEADS, HEAD_DIM), places).astype(jnp.bfloat16)
    values = mixed[:, query_width + KVW:]
    new_kv = jnp.concatenate([keys.reshape(ROWS, KVW), values], axis=1)
    attended = lax.map(attend, (query.reshape(N_TOK, ROWS_T, HEADS, HEAD_DIM), keys.reshape(N_TOK, ROWS_T, KV_HEADS, HEAD_DIM), values.reshape(N_TOK, ROWS_T, KV_HEADS, HEAD_DIM), k_cache.reshape(N_TOK, REQ_T, MAXLEN, KVW), v_cache.reshape(N_TOK, REQ_T, MAXLEN, KVW), owned)).reshape(ROWS, query_width)
    residual = hidden.astype(jnp.float32) + jnp.dot(attended, w_out, preferred_element_type=jnp.float32)
    middle = settle(residual)
    normed_ffn = norm_rows(middle, g_ffn)
    gate = jnp.dot(normed_ffn, w_gate, preferred_element_type=jnp.float32)
    up = jnp.dot(normed_ffn, w_up, preferred_element_type=jnp.float32)
    activated = (jax.nn.silu(gate) * up).astype(jnp.bfloat16)
    output = (residual + jnp.dot(activated, w_down, preferred_element_type=jnp.float32)).astype(jnp.bfloat16)
    return (output, new_kv)
```

```python
import jax
import jax.numpy as jnp
from jax import lax
from jax.experimental import pallas as pl
from jax.experimental.pallas import tpu as pltpu
from jax.sharding import PartitionSpec as P

D = 1280
HEADS = 20
KV_HEADS = 5
GROUPS = 4
HEAD_DIM = 64
HALF = 32
STRETCH = 512
DECODES = 16
ROWS = 528
SPAN = 128
WID = 16
QKV_OWN = 120
OWN = 80
FF_OWN = 224
KVW = 320
KEYS = SPAN + STRETCH // WID
BLOCK = 96

EPSILON = 1e-05
MASKED = -(2.0**100)
SCALE = 0.125
BF = jnp.bfloat16
F32 = jnp.float32


def dot(a, b, ca, cb):
    return lax.dot_general(a, b, (((ca,), (cb,)), ((), ())), preferred_element_type=F32)


def iota(shape, axis):
    return lax.broadcasted_iota(jnp.int32, shape, axis)


def split(x):
    high = x.astype(BF)
    return high, (x - high.astype(F32)).astype(BF)


def norm_cols(tall, gain):
    wide = tall.astype(F32)
    mean_square = jnp.sum(wide * wide, axis=0, keepdims=True) * (1.0 / D)
    return (wide * lax.rsqrt(mean_square + EPSILON) * gain).astype(BF)


def project_kernel(hidden, weight, gain, out):
    normed = norm_cols(hidden[...], gain[...])
    own = dot(weight[...], normed, 0, 0).astype(BF)
    for i in range(WID):
        out[i] = own


def turn(x, cosine, sine):
    first, second = x[:HALF], x[HALF:]
    return jnp.concatenate(
        [first * cosine - second * sine, second * cosine + first * sine], axis=0
    )


def attend_kernel(
    lens, place, mixed, cosine, sine, k_cache, v_cache, parts, fresh, keys, vals, bias, stats, outs, qb, sc, od
):
    w = place[0]
    cos_all, sin_all = cosine[...], sine[...]
    cos_p, sin_p = cos_all[:, :STRETCH], sin_all[:, :STRETCH]
    cos_d, sin_d = cos_all[:, STRETCH:], sin_all[:, STRETCH:]
    for g in range(KV_HEADS):
        at = D + HEAD_DIM * g
        fresh[HEAD_DIM * g : HEAD_DIM * (g + 1), :] = turn(
            mixed[at : at + HEAD_DIM, :].astype(F32), cos_all, sin_all
        ).astype(BF)
    fresh[KVW:, :] = mixed[D + KVW :, :]
    tile = fresh[:, pl.ds(pl.multiple_of(w // 4 * 128, 128), 128)].astype(F32)
    moved = pltpu.roll(tile, (128 - 32 * (w % 4)) % 128, 1)
    for g in range(KV_HEADS):
        rows = slice(HEAD_DIM * g, HEAD_DIM * (g + 1))
        keys[g, 0:SPAN, :] = k_cache[0, rows, :].astype(F32).T.astype(BF)
        keys[g, SPAN:KEYS, :] = moved[rows, :].T[: KEYS - SPAN].astype(BF)
    vals[:, 0:SPAN] = v_cache[0]
    vals[:, SPAN : 2 * SPAN] = moved[KVW:, :].astype(BF)
    spots = w * SPAN + iota((SPAN, STRETCH), 0)
    bias[0:SPAN, :] = jnp.where(spots < lens[0], 0.0, MASKED)
    later = iota((KEYS - SPAN, STRETCH), 1)
    earlier = w * (KEYS - SPAN) + iota((KEYS - SPAN, STRETCH), 0)
    bias[SPAN:KEYS, :] = jnp.where(earlier <= later, 0.0, MASKED)
    for h in range(HEADS):
        g = h // GROUPS
        query = turn(mixed[HEAD_DIM * h : HEAD_DIM * (h + 1), 0:STRETCH].astype(F32), cos_p, sin_p)
        query = (query.astype(BF).astype(F32) * SCALE).astype(BF)
        score = dot(keys[g], query, 1, 0) + bias[...]
        top, low = split(jnp.max(score, axis=0, keepdims=True))
        top, low = top.astype(F32), low.astype(F32)
        expo = jnp.exp(score - (top + low))
        total, rest = split(jnp.sum(expo, axis=0, keepdims=True))
        stats[0, h : h + 1, 0:STRETCH] = top
        stats[1, h : h + 1, 0:STRETCH] = low
        stats[2, h : h + 1, 0:STRETCH] = total.astype(F32)
        stats[3, h : h + 1, 0:STRETCH] = rest.astype(F32)
        outs[HEAD_DIM * h : HEAD_DIM * (h + 1), 0:STRETCH] = dot(
            vals[HEAD_DIM * g : HEAD_DIM * (g + 1), 0:KEYS], expo.astype(BF), 1, 0
        ).astype(BF)
    pick = (iota((128, DECODES), 0) // 8 == iota((128, DECODES), 1)).astype(BF)
    place_g = (iota((8, KVW), 0) == iota((8, KVW), 1) // HEAD_DIM).astype(F32)
    grid_mask = jnp.broadcast_to(place_g[None], (DECODES, 8, KVW)).reshape(128, KVW)
    k_self = dot(pick, fresh[0:KVW, STRETCH:ROWS], 1, 1)
    v_self = dot(pick, fresh[KVW:, STRETCH:ROWS], 1, 1)
    own_row = iota((128, 1), 0) // 8 == w
    self_score = []
    for k in range(GROUPS):
        pieces = []
        for g in range(KV_HEADS):
            at = HEAD_DIM * (GROUPS * g + k)
            pieces.append(
                turn(mixed[at : at + HEAD_DIM, STRETCH:ROWS].astype(F32), cos_d, sin_d)
            )
        tall = jnp.concatenate(pieces, axis=0).astype(BF)
        rows = dot(pick, tall, 1, 1) * grid_mask * SCALE
        qb[k] = rows
        self_score.append(
            jnp.where(own_row, jnp.sum(rows * k_self, axis=1, keepdims=True), MASKED)
        )
    for j in range(DECODES):
        query = jnp.concatenate([qb[k, 8 * j : 8 * j + 8, :] for k in range(GROUPS)], axis=0)
        score = dot(query.astype(BF), k_cache[j + 1], 1, 0)
        spots = w * SPAN + iota((32, SPAN), 1)
        score = jnp.where(spots < lens[j + 1], score, MASKED)
        for k in range(GROUPS):
            sc[k, 8 * j : 8 * j + 8, :] = score[8 * k : 8 * k + 8]
    lane = iota((128, 128), 1)
    group = iota((128, 128), 0) % 8
    table = jnp.zeros((128, 128), F32)
    self_weight = []
    for k in range(GROUPS):
        score = sc[k]
        top, low = split(jnp.maximum(jnp.max(score, axis=1, keepdims=True), self_score[k]))
        top, low = top.astype(F32), low.astype(F32)
        expo = jnp.exp(score - (top + low))
        own = jnp.exp(self_score[k] - (top + low))
        total, rest = split(jnp.sum(expo, axis=1, keepdims=True) + own)
        sc[k] = expo
        self_weight.append(own)
        for i, part in enumerate((top, low, total.astype(F32), rest.astype(F32))):
            table = jnp.where(lane == 32 * k + 8 * i + group, part, table)
    spread = (iota((128, 128), 0) // 8 == iota((128, 128), 1)).astype(BF)
    for j in range(DECODES):
        expo = jnp.concatenate([sc[k, 8 * j : 8 * j + 8, :] for k in range(GROUPS)], axis=0)
        summed = dot(expo.astype(BF), v_cache[j + 1], 1, 1)
        for k in range(GROUPS):
            od[k, 8 * j : 8 * j + 8, :] = summed[8 * k : 8 * k + 8]
    marks = dot(table.astype(BF), spread, 0, 0)
    for k in range(GROUPS):
        rows = ((od[k] + self_weight[k] * v_self) * grid_mask).astype(BF)
        tall = dot(rows, spread, 0, 0).astype(BF)
        for g in range(KV_HEADS):
            h = GROUPS * g + k
            outs[HEAD_DIM * h : HEAD_DIM * (h + 1), STRETCH:ROWS] = tall[
                HEAD_DIM * g : HEAD_DIM * (g + 1), 0:DECODES
            ]
            for i in range(4):
                at = 32 * k + 8 * i + g
                stats[i, h : h + 1, STRETCH:ROWS] = marks[at : at + 1, 0:DECODES]
    for i in range(WID):
        h = OWN * i // HEAD_DIM
        parts[i, 0:OWN, :] = outs[OWN * i : OWN * (i + 1), :]
        parts[i, OWN:BLOCK, :] = jnp.concatenate(
            [stats[n, h : h + 2, :] for n in range(4)] + [jnp.zeros((8, ROWS), F32)], axis=0
        ).astype(BF)


def merge_kernel(place, parts, out):
    w = place[0]
    second = (OWN * w) % HEAD_DIM + iota((OWN, ROWS), 0) >= HEAD_DIM
    peaks, totals = [], []
    for s in range(WID):
        marks = parts[s, OWN:BLOCK, :].astype(F32)
        peaks.append(marks[0:2] + marks[2:4])
        totals.append(marks[4:6] + marks[6:8])
    peak = peaks[0]
    for s in range(1, WID):
        peak = jnp.maximum(peak, peaks[s])
    shares = [jnp.exp(p - peak) for p in peaks]
    whole = shares[0] * totals[0]
    for s in range(1, WID):
        whole = whole + shares[s] * totals[s]
    total = jnp.zeros((OWN, ROWS), F32)
    for s in range(WID):
        share = shares[s] / whole
        total = total + jnp.where(second, share[1:2], share[0:1]) * parts[s, 0:OWN, :].astype(F32)
    own = total.astype(BF)
    for i in range(WID):
        out[i] = own


def out_kernel(attended, weight, hidden, residual, out):
    own = hidden[...].astype(F32) + dot(weight[...], attended[...], 1, 0)
    residual[...] = own
    middle = own.astype(BF)
    for i in range(WID):
        out[i] = middle


def ffn_kernel(middle, weight, down, gain, out):
    normed = norm_cols(middle[...], gain[...])
    both = dot(weight[...], normed, 1, 0)
    gate, up = both[:FF_OWN], both[FF_OWN:]
    act = (gate / (1.0 + jnp.exp(-gate)) * up).astype(BF)
    for i in range(WID):
        out[i] = dot(down[OWN * i : OWN * (i + 1), :], act, 1, 0).astype(BF)


def final_kernel(parts, residual, out):
    total = residual[...]
    for s in range(WID):
        total = total + parts[s].astype(F32)
    out[...] = total.astype(BF)


VMEM = pl.BlockSpec(memory_space=pltpu.VMEM)
SMEM = pl.BlockSpec(memory_space=pltpu.SMEM)
PARAMS = pltpu.CompilerParams(vmem_limit_bytes=56 * 1024 * 1024)


def call(kernel, outs, *args, scalars=0, scratch=(), flops=10**8):
    many = isinstance(outs, list)
    return pl.pallas_call(
        kernel,
        out_shape=outs,
        in_specs=[SMEM] * scalars + [VMEM] * (len(args) - scalars),
        out_specs=[VMEM] * len(outs) if many else VMEM,
        scratch_shapes=list(scratch),
        compiler_params=PARAMS,
        cost_estimate=pl.CostEstimate(flops=flops, bytes_accessed=4 * 10**6, transcendentals=0),
    )(*args)


def shape(*dims, dtype=BF):
    return jax.ShapeDtypeStruct(dims, dtype)


def shards(hidden, w_qkv, w_out, w_gate, w_up, w_down, g_attn, g_ffn, lengths, k_cache, v_cache):
    place = lax.axis_index("wid").astype(jnp.int32)
    place_arr = place.reshape(1)
    hidden_t = hidden.T

    def swap(blocks):
        return lax.all_to_all(blocks, "wid", 0, 0)

    all_hidden = swap(jnp.broadcast_to(hidden_t[None], (WID, OWN, ROWS))).reshape(D, ROWS)
    qkv = lax.all_gather(w_qkv, "tok", axis=0, tiled=True)
    rest = lax.all_gather(
        jnp.concatenate([w_gate, w_up, w_out, w_down.T], axis=1), "tok", axis=0, tiled=True
    )
    mixed = swap(
        call(
            project_kernel,
            shape(WID, QKV_OWN, ROWS),
            all_hidden,
            qkv,
            g_attn[:, None],
        )
    ).reshape(WID * QKV_OWN, ROWS)
    places = jnp.concatenate([lengths[0] + jnp.arange(STRETCH), lengths[1:]])
    ladder = jnp.arange(HALF).astype(F32) * (2.0 / HEAD_DIM)
    freqs = jnp.power(10000.0, -ladder)
    angles = freqs[:, None] * places.astype(F32)[None, :]
    parts, fresh = call(
        attend_kernel,
        [shape(WID, BLOCK, ROWS), shape(2 * KVW, ROWS)],
        lengths,
        place_arr,
        mixed,
        jnp.cos(angles),
        jnp.sin(angles),
        k_cache.transpose(0, 2, 1),
        v_cache.transpose(0, 2, 1),
        scalars=2,
        scratch=(
            pltpu.VMEM((KV_HEADS, KEYS, HEAD_DIM), BF),
            pltpu.VMEM((KVW, 2 * SPAN), BF),
            pltpu.VMEM((KEYS, STRETCH), F32),
            pltpu.VMEM((4, 24, ROWS), F32),
            pltpu.VMEM((D, ROWS), BF),
            pltpu.VMEM((GROUPS, 128, KVW), F32),
            pltpu.VMEM((GROUPS, 128, 128), F32),
            pltpu.VMEM((GROUPS, 128, KVW), F32),
        ),
    )
    new_kv = lax.dynamic_slice_in_dim(fresh, place * 40, 40, 0).T
    attended = swap(
        call(merge_kernel, shape(WID, OWN, ROWS), place_arr, swap(parts), scalars=1)
    ).reshape(D, ROWS)
    tall = rest[:, : 2 * FF_OWN + OWN].T
    gate_up, out_own = tall[: 2 * FF_OWN], tall[2 * FF_OWN :]
    down = rest[:, 2 * FF_OWN + OWN :]
    residual, middle = call(
        out_kernel,
        [shape(OWN, ROWS, dtype=F32), shape(WID, OWN, ROWS)],
        attended,
        out_own,
        hidden_t,
    )
    sums = swap(
        call(
            ffn_kernel,
            shape(WID, OWN, ROWS),
            swap(middle).reshape(D, ROWS),
            gate_up,
            down,
            g_ffn[:, None],
        )
    )
    output = call(final_kernel, shape(OWN, ROWS), sums, residual)
    return (output.T, new_kv)


def solution(mesh):
    placed = (
        P("tok", "wid"),
        P("tok", "wid"),
        P("tok", "wid"),
        P("tok", "wid"),
        P("tok", "wid"),
        P("wid", "tok"),
        P(),
        P(),
        P("tok"),
        P("tok", "wid", None),
        P("tok", "wid", None),
    )
    return jax.shard_map(
        shards,
        mesh=mesh,
        in_specs=placed,
        out_specs=(P("tok", "wid"), P("tok", "wid")),
        check_vma=False,
    )
```

```python
import jax
import jax.numpy as jnp
from jax import lax
from jax.experimental import pallas as pl
from jax.experimental.pallas import tpu as pltpu
from jax.sharding import PartitionSpec as P

D = 1280
HEADS = 20
KV_HEADS = 5
GROUPS = 4
HEAD_DIM = 64
HALF = 32
STRETCH = 512
DECODES = 16
ROWS = 528
SPAN = 128
WID = 16
QKV_OWN = 120
OWN = 80
FF_OWN = 224
KVW = 320
OLD = 4 * SPAN
KEYS = OLD + STRETCH // 4
FEATS = 320
BLOCK = 384
SEND = 352
QKV_SEND = 144

EPSILON = 1e-05
MASKED = -(2.0**100)
SCALE = 0.125
BF = jnp.bfloat16
F32 = jnp.float32


def dot(a, b, ca, cb):
    return lax.dot_general(a, b, (((ca,), (cb,)), ((), ())), preferred_element_type=F32)


def iota(shape, axis):
    return lax.broadcasted_iota(jnp.int32, shape, axis)


def split(x):
    high = x.astype(BF)
    return high, (x - high.astype(F32)).astype(BF)


def column(gain):
    square = jnp.concatenate([gain, jnp.zeros((118, 128), F32)], axis=0).T
    return jnp.concatenate([square[:, i : i + 1] for i in range(10)], axis=0)


def norm_cols(tall, gain):
    wide = tall.astype(F32)
    mean_square = jnp.sum(wide * wide, axis=0, keepdims=True) * (1.0 / D)
    return (wide * lax.rsqrt(mean_square + EPSILON) * gain).astype(BF)


def copies_kernel(block, out):
    own = block[...]
    for i in range(WID):
        out[i] = own


def project_kernel(place, hidden, weight, gain, out):
    w = place[0]
    normed = norm_cols(hidden[...], column(gain[...]))
    own = dot(weight[...], normed, 0, 0)
    same = (iota((QKV_OWN, 128), 0) == iota((QKV_OWN, 128), 1)).astype(BF)
    decoding = dot(own[:, STRETCH:ROWS].astype(BF), same, 0, 0).astype(BF)
    is_query = w * QKV_OWN + iota((QKV_OWN, 128), 0) < D
    pad = jnp.zeros((8, 128), F32)
    for y in range(4):
        for x in range(4):
            block = jnp.where(
                is_query, own[:, 128 * x : 128 * (x + 1)], own[:, 128 * y : 128 * (y + 1)]
            )
            out[4 * y + x, 0:128, :] = jnp.concatenate([block, pad], axis=0).astype(BF)
            out[4 * y + x, 128:QKV_SEND, :] = decoding


def turn(x, cosine, sine):
    first, second = x[:HALF], x[HALF:]
    return jnp.concatenate(
        [first * cosine - second * sine, second * cosine + first * sine], axis=0
    )


def decode_kernel(lens, place, mixed, waves, k_cache, v_cache, out, fresh, qb, sc, od):
    w = place[0]
    rows = jnp.concatenate(
        [mixed[i, 128:QKV_SEND, :].astype(F32)[:, :QKV_OWN] for i in range(WID)], axis=1
    )
    turned = rows[:, : D + KVW]
    ahead = pltpu.roll(turned, D + KVW - HALF, 1)
    behind = pltpu.roll(turned, HALF, 1)
    lane = iota((DECODES, D + KVW), 1) % HEAD_DIM
    cosine = jnp.concatenate([waves[0:DECODES, :]] * 13, axis=1)[:, : D + KVW]
    sine = jnp.concatenate([waves[DECODES : 2 * DECODES, :]] * 13, axis=1)[:, : D + KVW]
    turned = turned * cosine + jnp.where(lane < HALF, -ahead, behind) * sine
    turned = turned.astype(BF)
    both = jnp.concatenate([turned[:, D:].astype(F32), rows[:, D + KVW :]], axis=1).astype(BF)
    same = (iota((DECODES, 128), 0) == iota((DECODES, 128), 1)).astype(BF)
    fresh[...] = dot(both, same, 0, 0)[:, :DECODES].astype(BF)
    pick = (iota((128, DECODES), 0) // 8 == iota((128, DECODES), 1)).astype(BF)
    place_g = (iota((8, KVW), 0) == iota((8, KVW), 1) // HEAD_DIM).astype(F32)
    grid_mask = jnp.broadcast_to(place_g[None], (DECODES, 8, KVW)).reshape(128, KVW)
    selves = dot(pick, both, 1, 0)
    k_self, v_self = selves[:, :KVW], selves[:, KVW:]
    own_row = iota((128, 1), 0) // 8 == w
    wide = turned.astype(F32)
    self_score = []
    for k in range(GROUPS):
        part = jnp.concatenate(
            [
                wide[:, HEAD_DIM * (GROUPS * g + k) : HEAD_DIM * (GROUPS * g + k + 1)]
                for g in range(KV_HEADS)
            ],
            axis=1,
        )
        query = dot(pick, part.astype(BF), 1, 0) * grid_mask * SCALE
        qb[k] = query
        self_score.append(
            jnp.where(own_row, jnp.sum(query * k_self, axis=1, keepdims=True), MASKED)
        )
    for j in range(DECODES):
        query = jnp.concatenate([qb[k, 8 * j : 8 * j + 8, :] for k in range(GROUPS)], axis=0)
        score = dot(query.astype(BF), k_cache[j + 1], 1, 0)
        spots = w * SPAN + iota((32, SPAN), 1)
        score = jnp.where(spots < lens[j + 1], score, MASKED)
        for k in range(GROUPS):
            sc[k, 8 * j : 8 * j + 8, :] = score[8 * k : 8 * k + 8]
    lane = iota((128, 128), 1)
    group = iota((128, 128), 0) % 8
    table = jnp.zeros((128, 128), F32)
    self_weight = []
    for k in range(GROUPS):
        head = jnp.where(group < KV_HEADS, GROUPS * group + k, 100)
        score = sc[k]
        top, low = split(jnp.maximum(jnp.max(score, axis=1, keepdims=True), self_score[k]))
        top, low = top.astype(F32), low.astype(F32)
        expo = jnp.exp(score - (top + low))
        own = jnp.exp(self_score[k] - (top + low))
        total, rest = split(jnp.sum(expo, axis=1, keepdims=True) + own)
        sc[k] = expo
        self_weight.append(own)
        for i, part in enumerate((top, low, total.astype(F32), rest.astype(F32))):
            table = jnp.where(lane == head // 5 * 20 + 5 * i + head % 5, part, table)
    for j in range(DECODES):
        expo = jnp.concatenate([sc[k, 8 * j : 8 * j + 8, :] for k in range(GROUPS)], axis=0)
        summed = dot(expo.astype(BF), v_cache[j + 1], 1, 1)
        for k in range(GROUPS):
            od[k, 8 * j : 8 * j + 8, :] = summed[8 * k : 8 * k + 8]
    marks = dot(pick, table.astype(BF), 0, 0)
    flat = []
    for k in range(GROUPS):
        part = ((od[k] + self_weight[k] * v_self) * grid_mask).astype(BF)
        flat.append(dot(pick, part, 0, 0))
    decoded = jnp.concatenate(
        [flat[h % GROUPS][:, HEAD_DIM * (h // GROUPS) :][:, :HEAD_DIM] for h in range(HEADS)], axis=1
    )
    for y in range(4):
        block = jnp.concatenate(
            [
                decoded[:, FEATS * y : FEATS * (y + 1)],
                marks[:, 20 * y : 20 * (y + 1)],
                jnp.zeros((DECODES, 44), F32),
            ],
            axis=1,
        )
        for x in range(4):
            near = block[8 * (x // 2) : 8 * (x // 2) + 8]
            out[4 * y + x] = jnp.concatenate(
                [near[:, 128 * t : 128 * (t + 1)] for t in range(3)] + [jnp.zeros((8, 128), F32)],
                axis=0,
            ).astype(BF)


def prefill_kernel(lens, place, mixed, cosine, sine, caches, parts, tall, outs, fresh, keys, vals, bias, stats):
    w = place[0]
    y, x = w // 4, w % 4
    for i in range(WID):
        tall[QKV_OWN * i : QKV_OWN * (i + 1), :] = mixed[i, 0:128, :].astype(F32)[:QKV_OWN]
    cols_x = pl.ds(pl.multiple_of(x * 128, 128), 128)
    cols_y = pl.ds(pl.multiple_of(y * 128, 128), 128)
    cos_x, sin_x, cos_y, sin_y = cosine[:, cols_x], sine[:, cols_x], cosine[:, cols_y], sine[:, cols_y]
    for g in range(KV_HEADS):
        rows = slice(HEAD_DIM * g, HEAD_DIM * (g + 1))
        turned = turn(tall[D + HEAD_DIM * g : D + HEAD_DIM * (g + 1), :], cos_y, sin_y).astype(BF)
        fresh[rows, :] = turned.astype(F32)
        keys[g, OLD:KEYS, :] = turned.astype(F32).T.astype(BF)
        for i in range(4):
            keys[g, 128 * i : 128 * (i + 1), :] = caches[i, rows, :].astype(F32).T.astype(BF)
    fresh[KVW:, :] = tall[D + KVW :, :]
    for i in range(4):
        vals[:, 128 * i : 128 * (i + 1)] = caches[i, KVW:, :]
    vals[:, OLD:KEYS] = tall[D + KVW :, :].astype(BF)
    spots = y * OLD + iota((OLD, 128), 0)
    bias[0:OLD, :] = jnp.where(spots < lens[0], 0.0, MASKED)
    later = x * 128 + iota((128, 128), 1)
    earlier = y * 128 + iota((128, 128), 0)
    bias[OLD:KEYS, :] = jnp.where(earlier <= later, 0.0, MASKED)
    stats[...] = jnp.zeros(stats.shape, F32)
    for g in range(KV_HEADS):
        queries = []
        for k in range(GROUPS):
            at = HEAD_DIM * (GROUPS * g + k)
            query = turn(tall[at : at + HEAD_DIM, :], cos_x, sin_x)
            queries.append((query.astype(BF).astype(F32) * SCALE).astype(BF))
        scores = dot(keys[g], jnp.concatenate(queries, axis=1), 1, 0)
        expos = []
        for k in range(GROUPS):
            h = GROUPS * g + k
            score = scores[:, 128 * k : 128 * (k + 1)] + bias[...]
            top, low = split(jnp.max(score, axis=0, keepdims=True))
            top, low = top.astype(F32), low.astype(F32)
            expo = jnp.exp(score - (top + low))
            total, rest = split(jnp.sum(expo, axis=0, keepdims=True))
            for i, part in enumerate((top, low, total.astype(F32), rest.astype(F32))):
                at = 24 * (h // 5) + 5 * i + h % 5
                stats[at : at + 1, :] = part
            expos.append(expo.astype(BF))
        summed = dot(
            vals[HEAD_DIM * g : HEAD_DIM * (g + 1), :], jnp.concatenate(expos, axis=1), 1, 0
        ).astype(BF)
        for k in range(GROUPS):
            h = GROUPS * g + k
            outs[HEAD_DIM * h : HEAD_DIM * (h + 1), :] = summed[:, 128 * k : 128 * (k + 1)]
    for i in range(4):
        parts[i, 0:FEATS, :] = outs[FEATS * i : FEATS * (i + 1), :]
        at = pl.multiple_of(40 * (4 * i + x), 8)
        parts[i, FEATS:BLOCK, :] = jnp.concatenate(
            [stats[24 * i : 24 * i + 24, :], fresh[pl.ds(at, 40), :]], axis=0
        ).astype(BF)


def merge_shares(peaks, totals):
    peak = peaks[0]
    for p in peaks[1:]:
        peak = jnp.maximum(peak, p)
    shares = [jnp.exp(p - peak) for p in peaks]
    whole = shares[0] * totals[0]
    for share, total in zip(shares[1:], totals[1:]):
        whole = whole + share * total
    inverse = 1.0 / whole
    return [share * inverse for share in shares]


def tiles(rows):
    wide = jnp.concatenate([rows, jnp.zeros((8, 384 - FEATS), F32)], axis=1)
    return [wide[:, 128 * t : 128 * (t + 1)] for t in range(3)]


def merge_kernel(early, parts, decodes, out, fresh):
    extra = [parts[s, FEATS:BLOCK, :].astype(F32) for s in range(4)]
    shares = merge_shares(
        [m[0:5] + m[5:10] for m in extra], [m[10:15] + m[15:20] for m in extra]
    )
    for s in range(4):
        fresh[:, 128 * s : 128 * (s + 1)] = extra[s][24:64]
    own = []
    for i in range(5):
        total = jnp.zeros((HEAD_DIM, 128), F32)
        for s in range(4):
            total = total + shares[s][i : i + 1] * parts[
                s, HEAD_DIM * i : HEAD_DIM * (i + 1), :
            ].astype(F32)
        own.append(total.astype(BF))
    near = [decodes[s].astype(F32) for s in range(WID)]
    marks = [n[16:24, 64:84] for n in near]
    shares = merge_shares(
        [m[:, 0:5] + m[:, 5:10] for m in marks], [m[:, 10:15] + m[:, 15:20] for m in marks]
    )
    low = iota((8, 128), 1) < HEAD_DIM
    decoded = [jnp.zeros((8, 128), F32) for t in range(3)]
    for s in range(WID):
        for t in range(3):
            share = shares[s][:, 2 * t : 2 * t + 1]
            if t < 2:
                share = jnp.where(low, share, shares[s][:, 2 * t + 1 : 2 * t + 2])
            decoded[t] = decoded[t] + share * near[s][8 * t : 8 * t + 8]
    decoded[2] = jnp.where(low, decoded[2], 0.0)
    tail = jnp.concatenate(decoded + [jnp.zeros((8, 128), F32)], axis=0).astype(BF)
    for y in range(4):
        for i in range(5):
            out[y, HEAD_DIM * i : HEAD_DIM * (i + 1), :] = own[i]
        out[y, FEATS:SEND, :] = tail


def rows_of(blocks, index):
    tail = blocks[index, FEATS:SEND, :].astype(F32)
    return [tail[0:8], tail[8:16], tail[16:24, :HEAD_DIM]]


def out_kernel(place, attended, weight, hidden, hidden_dec, out):
    x = place[0] % 4
    tall = jnp.concatenate([attended[y, 0:FEATS, :] for y in range(4)], axis=0)
    own = hidden[...].astype(F32) + dot(weight[...], tall, 1, 0)
    rows = jnp.concatenate([t for y in range(4) for t in rows_of(attended, y)], axis=1)
    pick = (iota((8, DECODES), 1) == x // 2 * 8 + iota((8, DECODES), 0)).astype(BF)
    own_rows = dot(pick, hidden_dec[...], 1, 1) + dot(rows.astype(BF), weight[...], 1, 1)
    tail = jnp.concatenate(tiles(own_rows) + [jnp.zeros((8, 128), F32)], axis=0).astype(BF)
    middle = own.astype(BF)
    for i in range(WID):
        out[i, 0:FEATS, :] = middle
        out[i, FEATS:SEND, :] = tail


def ffn_kernel(place, blocks, weight, down, gain, out, residual, middle):
    w = place[0]
    for y in range(4):
        for x in range(4):
            middle[FEATS * y : FEATS * (y + 1), 128 * x : 128 * (x + 1)] = blocks[4 * y + x, 0:FEATS, :]
    rows = jnp.concatenate(
        [
            jnp.concatenate([t for y in range(4) for t in rows_of(blocks, 4 * y + x)], axis=1)
            for x in (0, 2)
        ],
        axis=0,
    )
    same = (iota((DECODES, DECODES), 0) == iota((DECODES, DECODES), 1)).astype(BF)
    middle[:, STRETCH:ROWS] = dot(rows.astype(BF), same, 0, 0).astype(BF)
    residual[...] = middle[pl.ds(pl.multiple_of(w * OWN, OWN), OWN), :]
    normed = norm_cols(middle[...], column(gain[...]))
    both = dot(weight[...], normed, 1, 0)
    gate, up = both[:FF_OWN], both[FF_OWN:]
    act = (gate / (1.0 + jnp.exp(-gate)) * up).astype(BF)
    for i in range(4):
        part = dot(down[FEATS * i : FEATS * (i + 1), :], act, 1, 0).astype(BF)
        for j in range(4):
            out[4 * i + j] = part[OWN * j : OWN * (j + 1)]


def final_kernel(parts, residual, out):
    total = residual[...].astype(F32)
    for s in range(WID):
        total = total + parts[s].astype(F32)
    out[...] = total.astype(BF)


VMEM = pl.BlockSpec(memory_space=pltpu.VMEM)
SMEM = pl.BlockSpec(memory_space=pltpu.SMEM)
ANY = pl.BlockSpec(memory_space=pl.ANY)


def call(kernel, outs, *args, scalars=0, anys=0, scratch=(), mib=16):
    many = isinstance(outs, list)
    return pl.pallas_call(
        kernel,
        out_shape=outs,
        in_specs=[SMEM] * scalars + [ANY] * anys + [VMEM] * (len(args) - scalars - anys),
        out_specs=[VMEM] * len(outs) if many else VMEM,
        scratch_shapes=list(scratch),
        compiler_params=pltpu.CompilerParams(vmem_limit_bytes=mib * 1024 * 1024),
        cost_estimate=pl.CostEstimate(flops=10**8, bytes_accessed=4 * 10**6, transcendentals=0),
    )(*args)


def shape(*dims, dtype=BF):
    return jax.ShapeDtypeStruct(dims, dtype)


def shards(hidden, w_qkv, w_out, w_gate, w_up, w_down, g_attn, g_ffn, lengths, k_cache, v_cache):
    y, x = lax.axis_index("y"), lax.axis_index("x")
    place = (4 * y + x).astype(jnp.int32).reshape(1)
    hidden_t = hidden.T

    def swap(blocks):
        return lax.all_to_all(blocks, ("y", "x"), 0, 0)

    all_hidden = swap(call(copies_kernel, shape(WID, OWN, ROWS), hidden_t)).reshape(D, ROWS)
    qkv = lax.all_gather(lax.all_gather(w_qkv, "core", axis=0, tiled=True), "z", axis=0, tiled=True)
    rest = lax.all_gather(
        jnp.concatenate([w_gate, w_up, w_out, w_down.T], axis=1),
        ("z", "core"),
        axis=0,
        tiled=True,
    )
    tall = rest[:, : 2 * FF_OWN + OWN].T
    gate_up = tall[: 2 * FF_OWN]
    out_own = lax.all_gather(tall[2 * FF_OWN :], "x", axis=0, tiled=True)
    down = rest[:, 2 * FF_OWN + OWN :]
    mixed = swap(
        call(
            project_kernel,
            shape(WID, QKV_SEND, 128),
            place,
            all_hidden,
            qkv,
            g_attn.reshape(10, 128),
            scalars=1,
        )
    )
    k_tall, v_tall = k_cache.transpose(0, 2, 1), v_cache.transpose(0, 2, 1)
    caches = lax.all_gather(
        jnp.concatenate([k_tall[0], v_tall[0]], axis=0), "x", axis=0, tiled=True
    ).reshape(4, 2 * KVW, SPAN)
    places = jnp.concatenate([lengths[0] + jnp.arange(STRETCH), lengths[1:]]).astype(F32)
    ladder = jnp.arange(HALF).astype(F32) * (2.0 / HEAD_DIM)
    freqs = jnp.power(10000.0, -ladder)
    angles = freqs[:, None] * places[None, :STRETCH]
    flat = places[STRETCH:, None] * jnp.concatenate([freqs] * 4)[None, :]
    decodes, fresh_decode = call(
        decode_kernel,
        [shape(WID, 32, 128), shape(2 * KVW, DECODES)],
        lengths,
        place,
        mixed,
        jnp.concatenate([jnp.cos(flat), jnp.sin(flat)], axis=0),
        k_tall,
        v_tall,
        scalars=2,
        scratch=(
            pltpu.VMEM((GROUPS, 128, KVW), F32),
            pltpu.VMEM((GROUPS, 128, 128), F32),
            pltpu.VMEM((GROUPS, 128, KVW), F32),
        ),
    )
    decodes = swap(decodes)
    parts = call(
        prefill_kernel,
        shape(4, BLOCK, 128),
        lengths,
        place,
        mixed,
        jnp.cos(angles),
        jnp.sin(angles),
        caches,
        scalars=2,
        scratch=(
            pltpu.VMEM((WID * QKV_OWN, 128), F32),
            pltpu.VMEM((D, 128), BF),
            pltpu.VMEM((2 * KVW, 128), F32),
            pltpu.VMEM((KV_HEADS, KEYS, HEAD_DIM), BF),
            pltpu.VMEM((KVW, KEYS), BF),
            pltpu.VMEM((KEYS, 128), F32),
            pltpu.VMEM((96, 128), F32),
        ),
    )
    attended, fresh_own = call(
        merge_kernel,
        [shape(4, SEND, 128), shape(40, STRETCH, dtype=F32)],
        out_own,
        lax.all_to_all(parts, "y", 0, 0),
        decodes,
        anys=1,
    )
    attended = lax.all_to_all(attended, "y", 0, 0)
    new_kv = jnp.concatenate(
        [
            fresh_own.astype(BF),
            lax.dynamic_slice_in_dim(fresh_decode, place[0] * 40, 40, 0),
        ],
        axis=1,
    ).T
    own_hidden = lax.dynamic_slice(all_hidden, (FEATS * y, 128 * x), (FEATS, 128))
    own_decode = lax.dynamic_slice(all_hidden, (FEATS * y, STRETCH), (FEATS, DECODES))
    middle = call(
        out_kernel,
        shape(WID, SEND, 128),
        place,
        attended,
        out_own,
        own_hidden,
        own_decode,
        scalars=1,
    )
    sums, residual = call(
        ffn_kernel,
        [shape(WID, OWN, ROWS), shape(OWN, ROWS)],
        place,
        swap(middle),
        gate_up,
        down,
        g_ffn.reshape(10, 128),
        scalars=1,
        mib=24,
        scratch=(pltpu.VMEM((D, ROWS), BF),),
    )
    output = call(final_kernel, shape(OWN, ROWS), swap(sums), residual)
    return (output.T, new_kv)


def solution(mesh):
    core = 2 if mesh.shape["tok"] % 2 == 0 else 1
    devices = mesh.devices.reshape(mesh.shape["tok"] // core, core, 4, 4)
    finer = jax.sharding.Mesh(devices, ("z", "core", "y", "x"))
    tok, wid = ("z", "core"), ("y", "x")
    placed = (
        P(tok, wid),
        P(tok, wid),
        P(tok, wid),
        P(tok, wid),
        P(tok, wid),
        P(wid, tok),
        P(),
        P(),
        P(tok),
        P(tok, wid, None),
        P(tok, wid, None),
    )
    return jax.shard_map(
        shards,
        mesh=finer,
        in_specs=placed,
        out_specs=(P(tok, wid), P(tok, wid)),
        check_vma=False,
    )
```

```python
import jax
import jax.numpy as jnp
from jax import lax
from jax.experimental import pallas as pl
from jax.experimental.pallas import tpu as pltpu
from jax.sharding import PartitionSpec as P

D = 1280
HEADS = 20
KV_HEADS = 5
GROUPS = 4
HEAD_DIM = 64
HALF = 32
STRETCH = 512
DECODES = 16
ROWS = 528
SPAN = 128
WID = 16
QKV_OWN = 120
OWN = 80
FF_OWN = 224
KVW = 320
OLD = 4 * SPAN
KEYS = OLD + STRETCH // 4
FEATS = 320
BLOCK = 1408
TAIL = 1360
SEND = 352
QKV_SEND = 304
WIDE = 640
PIECE = 40

EPSILON = 1e-05
MASKED = -(2.0**100)
SCALE = 0.125
BF = jnp.bfloat16
F32 = jnp.float32


def dot(a, b, ca, cb):
    return lax.dot_general(a, b, (((ca,), (cb,)), ((), ())), preferred_element_type=F32)


def iota(shape, axis):
    return lax.broadcasted_iota(jnp.int32, shape, axis)


def split(x):
    high = x.astype(BF)
    return high, (x - high.astype(F32)).astype(BF)


def column(gain):
    square = jnp.concatenate([gain, jnp.zeros((118, 128), F32)], axis=0).T
    return jnp.concatenate([square[:, i : i + 1] for i in range(10)], axis=0)


def norm_cols(tall, gain):
    wide = tall.astype(F32)
    mean_square = jnp.sum(wide * wide, axis=0, keepdims=True) * (1.0 / D)
    return (wide * lax.rsqrt(mean_square + EPSILON) * gain).astype(BF)


def ship(pairs, sems):
    moves = [pltpu.make_async_copy(a, b, sems.at[i]) for i, (a, b) in enumerate(pairs)]
    for move in moves:
        move.start()
    for move in moves:
        move.wait()


def start_kernel(hidden_far, k_far, v_far, far, hidden, cache, out, sems):
    ship(
        [
            (hidden_far, hidden),
            (k_far.at[0], cache.at[pl.ds(0, KVW)]),
            (v_far.at[0], cache.at[pl.ds(KVW, KVW)]),
        ],
        sems,
    )
    main = hidden[:, 0:STRETCH]
    ending = hidden[:, STRETCH:ROWS].astype(F32)
    wide = cache[...].astype(F32)
    pad = jnp.zeros((OWN, 128 - DECODES - HEAD_DIM), F32)
    moves = []
    for i in range(WID):
        piece = wide[PIECE * i : PIECE * (i + 1)]
        halves = jnp.concatenate([piece[:, :HEAD_DIM], piece[:, HEAD_DIM:]], axis=0)
        out[i, :, 0:STRETCH] = main
        out[i, :, STRETCH:WIDE] = jnp.concatenate([ending, halves, pad], axis=1).astype(BF)
        moves.append(pltpu.make_async_copy(out.at[i], far.at[i], sems.at[3 + i]))
        moves[i].start()
    for move in moves:
        move.wait()


def first_kernel(qkv, out):
    out[...] = jnp.concatenate(
        [qkv[...].astype(F32), jnp.zeros((out.shape[0], 8), F32)], axis=1
    ).astype(BF)


def second_kernel(gate, up, down, projection, out):
    for i, ref in enumerate((gate, up, down)):
        out[:, 256 * i : 256 * (i + 1)] = jnp.concatenate(
            [ref[...].astype(F32), jnp.zeros((out.shape[0], 32), F32)], axis=1
        ).astype(BF)
    out[:, 768:896] = jnp.concatenate(
        [projection[...].astype(F32), jnp.zeros((out.shape[0], 48), F32)], axis=1
    ).astype(BF)


def tall_kernel(early, far, out, weight, sems):
    ship([(far.at[:, pl.ds(768, 128)], weight)], sems)
    out[...] = weight[...].astype(F32).T[:OWN].astype(BF)


def project_kernel(place, hidden, weight, gain, far, out, sems):
    w = place[0]
    normed = norm_cols(hidden[:, 0:ROWS], column(gain[...]))
    own = dot(weight[...], normed, 0, 0)
    same = (iota((128, 128), 0) == iota((128, 128), 1)).astype(BF)
    decoding = dot(own[:, STRETCH:ROWS].astype(BF), same, 0, 0).astype(BF)
    is_query = w * QKV_OWN + iota((128, 128), 0) < D
    for y in range(4):
        pieces = []
        for x in range(4):
            i = 4 * y + x
            ending = hidden[OWN * i : OWN * (i + 1), STRETCH:WIDE].astype(F32)
            ending = ending[:, DECODES : DECODES + HEAD_DIM]
            pieces.append(jnp.concatenate([ending[:PIECE], ending[PIECE:]], axis=1))
        caches = jnp.concatenate(pieces, axis=0).astype(BF)
        for x in range(4):
            block = jnp.where(
                is_query, own[:, 128 * x : 128 * (x + 1)], own[:, 128 * y : 128 * (y + 1)]
            )
            out[4 * y + x, 0:128, :] = block.astype(BF)
            out[4 * y + x, 128:144, :] = decoding
            out[4 * y + x, 144:QKV_SEND, :] = caches
    ship([(out, far)], sems)


def turn(x, cosine, sine):
    first, second = x[:HALF], x[HALF:]
    return jnp.concatenate(
        [first * cosine - second * sine, second * cosine + first * sine], axis=0
    )


def decode_kernel(lens, place, k_far, v_far, mixed, waves, far, fresh_far, out, fresh, qb, sc, od, k_cache, v_cache, sems):
    w = place[0]
    k_move = pltpu.make_async_copy(k_far.at[pl.ds(1, DECODES)], k_cache, sems.at[0, 0])
    v_move = pltpu.make_async_copy(v_far.at[pl.ds(1, DECODES)], v_cache, sems.at[0, 1])
    k_move.start()
    v_move.start()
    rows = jnp.concatenate(
        [mixed[i, 128:144, :].astype(F32)[:, :QKV_OWN] for i in range(WID)], axis=1
    )
    turned = rows[:, : D + KVW]
    ahead = pltpu.roll(turned, D + KVW - HALF, 1)
    behind = pltpu.roll(turned, HALF, 1)
    lane = iota((DECODES, D + KVW), 1) % HEAD_DIM
    cosine = jnp.concatenate([waves[0:DECODES, :]] * 13, axis=1)[:, : D + KVW]
    sine = jnp.concatenate([waves[DECODES : 2 * DECODES, :]] * 13, axis=1)[:, : D + KVW]
    turned = turned * cosine + jnp.where(lane < HALF, -ahead, behind) * sine
    turned = turned.astype(BF)
    both = jnp.concatenate([turned[:, D:].astype(F32), rows[:, D + KVW :]], axis=1).astype(BF)
    same = (iota((DECODES, 128), 0) == iota((DECODES, 128), 1)).astype(BF)
    fresh[...] = dot(both, same, 0, 0)
    pick = (iota((128, DECODES), 0) // 8 == iota((128, DECODES), 1)).astype(BF)
    place_g = (iota((8, KVW), 0) == iota((8, KVW), 1) // HEAD_DIM).astype(F32)
    grid_mask = jnp.broadcast_to(place_g[None], (DECODES, 8, KVW)).reshape(128, KVW)
    selves = dot(pick, both, 1, 0)
    k_self, v_self = selves[:, :KVW], selves[:, KVW:]
    own_row = iota((128, 1), 0) // 8 == w
    wide = turned.astype(F32)
    self_score = []
    for k in range(GROUPS):
        part = jnp.concatenate(
            [
                wide[:, HEAD_DIM * (GROUPS * g + k) : HEAD_DIM * (GROUPS * g + k + 1)]
                for g in range(KV_HEADS)
            ],
            axis=1,
        )
        query = dot(pick, part.astype(BF), 1, 0) * grid_mask * SCALE
        qb[k] = query
        self_score.append(
            jnp.where(own_row, jnp.sum(query * k_self, axis=1, keepdims=True), MASKED)
        )
    k_move.wait()
    for j in range(DECODES):
        query = jnp.concatenate([qb[k, 8 * j : 8 * j + 8, :] for k in range(GROUPS)], axis=0)
        score = dot(query.astype(BF), k_cache[j], 1, 0)
        spots = w * SPAN + iota((32, SPAN), 1)
        score = jnp.where(spots < lens[j + 1], score, MASKED)
        for k in range(GROUPS):
            sc[k, 8 * j : 8 * j + 8, :] = score[8 * k : 8 * k + 8]
    lane = iota((128, 128), 1)
    group = iota((128, 128), 0) % 8
    table = jnp.zeros((128, 128), F32)
    self_weight = []
    for k in range(GROUPS):
        head = jnp.where(group < KV_HEADS, GROUPS * group + k, 1000)
        score = sc[k]
        top, low = split(jnp.maximum(jnp.max(score, axis=1, keepdims=True), self_score[k]))
        top, low = top.astype(F32), low.astype(F32)
        expo = jnp.exp(score - (top + low))
        own = jnp.exp(self_score[k] - (top + low))
        total, rest = split(jnp.sum(expo, axis=1, keepdims=True) + own)
        sc[k] = expo
        self_weight.append(own)
        for i, part in enumerate((top, low, total.astype(F32), rest.astype(F32))):
            table = jnp.where(lane == HEADS * i + head, part, table)
    v_move.wait()
    for j in range(DECODES):
        expo = jnp.concatenate([sc[k, 8 * j : 8 * j + 8, :] for k in range(GROUPS)], axis=0)
        summed = dot(expo.astype(BF), v_cache[j], 1, 1)
        for k in range(GROUPS):
            od[k, 8 * j : 8 * j + 8, :] = summed[8 * k : 8 * k + 8]
    marks = dot(pick, table.astype(BF), 0, 0)
    flat = []
    for k in range(GROUPS):
        part = ((od[k] + self_weight[k] * v_self) * grid_mask).astype(BF)
        flat.append(dot(pick, part, 0, 0))
    decoded = jnp.concatenate(
        [flat[h % GROUPS][:, HEAD_DIM * (h // GROUPS) :][:, :HEAD_DIM] for h in range(HEADS)], axis=1
    )
    for half in range(2):
        rows = slice(8 * half, 8 * half + 8)
        block = jnp.concatenate(
            [decoded[rows, 128 * t : 128 * (t + 1)] for t in range(10)]
            + [marks[rows], jnp.zeros((8, 128), F32)],
            axis=0,
        ).astype(BF)
        out[half] = block
    at = pl.multiple_of(40 * w, 8)
    ship(
        [(out.at[i % 4 // 2], far.at[i]) for i in range(WID)] + [(fresh.at[pl.ds(at, 40)], fresh_far)],
        sems.at[1],
    )


def prefill_kernel(lens, place, mixed, cosine, sine, far, tall, fresh, keys, vals, bias, stats, parts, tails, sems):
    w = place[0]
    y, x = w // 4, w % 4
    for i in range(WID):
        tall[QKV_OWN * i : QKV_OWN * (i + 1), :] = mixed[i, 0:128, :].astype(F32)[:QKV_OWN]
    old = [mixed[i, 144:QKV_SEND, :].astype(F32) for i in range(WID)]
    caches = [
        jnp.concatenate([o[PIECE * i : PIECE * (i + 1)] for o in old], axis=0) for i in range(4)
    ]
    cols_x = pl.ds(pl.multiple_of(x * 128, 128), 128)
    cols_y = pl.ds(pl.multiple_of(y * 128, 128), 128)
    cos_x, sin_x, cos_y, sin_y = cosine[:, cols_x], sine[:, cols_x], cosine[:, cols_y], sine[:, cols_y]
    for g in range(KV_HEADS):
        rows = slice(HEAD_DIM * g, HEAD_DIM * (g + 1))
        turned = turn(tall[D + HEAD_DIM * g : D + HEAD_DIM * (g + 1), :], cos_y, sin_y).astype(BF)
        fresh[rows, :] = turned.astype(F32)
        keys[g, OLD:KEYS, :] = turned.astype(F32).T.astype(BF)
        for i in range(4):
            keys[g, 128 * i : 128 * (i + 1), :] = caches[i][rows].T.astype(BF)
    fresh[KVW:, :] = tall[D + KVW :, :]
    for i in range(4):
        vals[:, 128 * i : 128 * (i + 1)] = caches[i][KVW:].astype(BF)
    vals[:, OLD:KEYS] = tall[D + KVW :, :].astype(BF)
    spots = y * OLD + iota((OLD, 128), 0)
    bias[0:OLD, :] = jnp.where(spots < lens[0], 0.0, MASKED)
    later = x * 128 + iota((128, 128), 1)
    earlier = y * 128 + iota((128, 128), 0)
    bias[OLD:KEYS, :] = jnp.where(earlier <= later, 0.0, MASKED)
    for g in range(KV_HEADS):
        queries = []
        for k in range(GROUPS):
            at = HEAD_DIM * (GROUPS * g + k)
            query = turn(tall[at : at + HEAD_DIM, :], cos_x, sin_x)
            queries.append((query.astype(BF).astype(F32) * SCALE).astype(BF))
        scores = dot(keys[g], jnp.concatenate(queries, axis=1), 1, 0)
        expos = []
        for k in range(GROUPS):
            h = GROUPS * g + k
            score = scores[:, 128 * k : 128 * (k + 1)] + bias[...]
            top, low = split(jnp.max(score, axis=0, keepdims=True))
            top, low = top.astype(F32), low.astype(F32)
            expo = jnp.exp(score - (top + low))
            total, rest = split(jnp.sum(expo, axis=0, keepdims=True))
            for i, part in enumerate((top, low, total.astype(F32), rest.astype(F32))):
                stats[HEADS * i + h : HEADS * i + h + 1, :] = part
            expos.append(expo.astype(BF))
        summed = dot(
            vals[HEAD_DIM * g : HEAD_DIM * (g + 1), :], jnp.concatenate(expos, axis=1), 1, 0
        ).astype(BF)
        for k in range(GROUPS):
            h = GROUPS * g + k
            parts[HEAD_DIM * h : HEAD_DIM * (h + 1), :] = summed[:, 128 * k : 128 * (k + 1)]
    parts[D:TAIL, :] = stats[...].astype(BF)
    for i in range(4):
        at = pl.multiple_of(40 * (4 * i + x), 8)
        tails[i] = jnp.concatenate([fresh[pl.ds(at, 40), :], jnp.zeros((8, 128), F32)], axis=0).astype(BF)
    ship(
        [(parts, far.at[i, pl.ds(0, TAIL)]) for i in range(4)]
        + [(tails.at[i], far.at[i, pl.ds(TAIL, BLOCK - TAIL)]) for i in range(4)],
        sems,
    )


def merge_shares(peaks, totals):
    peak = peaks[0]
    for p in peaks[1:]:
        peak = jnp.maximum(peak, p)
    shares = [jnp.exp(p - peak) for p in peaks]
    whole = shares[0] * totals[0]
    for share, total in zip(shares[1:], totals[1:]):
        whole = whole + share * total
    inverse = 1.0 / whole
    return [share * inverse for share in shares]


def tiles(rows):
    wide = jnp.concatenate([rows, jnp.zeros((8, 384 - FEATS), F32)], axis=1)
    return [wide[:, 128 * t : 128 * (t + 1)] for t in range(3)]


def rows_of(blocks, index):
    tail = blocks[index, FEATS:SEND, :].astype(F32)
    return [tail[0:8], tail[8:16], tail[16:24, :HEAD_DIM]]


def merge_kernel(place, parts, decodes, weight, hidden, hidden_dec, far, fresh_far, tall, out, fresh, sems):
    x = place[0] % 4
    extra = [parts[s, D:BLOCK, :].astype(F32) for s in range(4)]
    shares = merge_shares(
        [m[0:20] + m[20:40] for m in extra], [m[40:60] + m[60:80] for m in extra]
    )
    for s in range(4):
        fresh[:, 128 * s : 128 * (s + 1)] = extra[s][80:120]
    for h in range(HEADS):
        rows = slice(HEAD_DIM * h, HEAD_DIM * (h + 1))
        total = shares[0][h : h + 1] * parts[0, rows, :].astype(F32)
        for s in range(1, 4):
            total = total + shares[s][h : h + 1] * parts[s, rows, :].astype(F32)
        tall[rows, :] = total.astype(BF)
    own = hidden[...].astype(F32) + dot(weight[...], tall[...], 1, 0)
    near = [decodes[s].astype(F32) for s in range(WID)]
    marks = [n[80:88] for n in near]
    shares = merge_shares(
        [m[:, 0:20] + m[:, 20:40] for m in marks], [m[:, 40:60] + m[:, 60:80] for m in marks]
    )
    low = iota((8, 128), 1) < HEAD_DIM
    decoded = [jnp.zeros((8, 128), F32) for t in range(10)]
    for s in range(WID):
        for t in range(10):
            share = jnp.where(low, shares[s][:, 2 * t : 2 * t + 1], shares[s][:, 2 * t + 1 : 2 * t + 2])
            decoded[t] = decoded[t] + share * near[s][8 * t : 8 * t + 8]
    rows = jnp.concatenate(decoded, axis=1).astype(BF)
    pick = (iota((8, DECODES), 1) == x // 2 * 8 + iota((8, DECODES), 0)).astype(BF)
    own_rows = dot(pick, hidden_dec[...], 1, 1) + dot(rows, weight[...], 1, 1)
    tail = jnp.concatenate(tiles(own_rows) + [jnp.zeros((8, 128), F32)], axis=0).astype(BF)
    out[0:FEATS, :] = own.astype(BF)
    out[FEATS:SEND, :] = tail
    ship([(out, far.at[i]) for i in range(WID)] + [(fresh, fresh_far)], sems)


def ffn_kernel(place, far_weight, far_down, blocks, gain, far, residual, middle, weight, down, out, sems):
    w = place[0]
    weight_move = pltpu.make_async_copy(far_weight, weight, sems.at[0])
    down_move = pltpu.make_async_copy(far_down, down, sems.at[1])
    weight_move.start()
    down_move.start()
    for y in range(4):
        for x in range(4):
            middle[FEATS * y : FEATS * (y + 1), 128 * x : 128 * (x + 1)] = blocks[4 * y + x, 0:FEATS, :]
    rows = jnp.concatenate(
        [
            jnp.concatenate([t for y in range(4) for t in rows_of(blocks, 4 * y + x)], axis=1)
            for x in (0, 2)
        ],
        axis=0,
    )
    same = (iota((DECODES, DECODES), 0) == iota((DECODES, DECODES), 1)).astype(BF)
    middle[:, STRETCH:ROWS] = dot(rows.astype(BF), same, 0, 0).astype(BF)
    residual[...] = middle[pl.ds(pl.multiple_of(w * OWN, OWN), OWN), :]
    normed = norm_cols(middle[...], column(gain[...]))
    weight_move.wait()
    both = dot(weight[...], normed, 1, 0)
    gate, up = both[:FF_OWN], both[FF_OWN:]
    act = (gate / (1.0 + jnp.exp(-gate)) * up).astype(BF)
    down_move.wait()
    moves = []
    for i in range(4):
        part = dot(down[FEATS * i : FEATS * (i + 1), :], act, 1, 0).astype(BF)
        for j in range(4):
            out[4 * i + j] = part[OWN * j : OWN * (j + 1)]
        rows = pl.ds(4 * i, 4)
        moves.append(pltpu.make_async_copy(out.at[rows], far.at[rows], sems.at[2 + i]))
        moves[i].start()
    for move in moves:
        move.wait()


def final_kernel(parts, residual, out):
    total = residual[...].astype(F32)
    for s in range(WID):
        total = total + parts[s].astype(F32)
    out[...] = total.astype(BF)


VMEM = pl.BlockSpec(memory_space=pltpu.VMEM)
SMEM = pl.BlockSpec(memory_space=pltpu.SMEM)
ANY = pl.BlockSpec(memory_space=pltpu.HBM)


def call(kernel, outs, *args, scalars=0, anys=0, scratch=(), mib=16, far=False):
    many = isinstance(outs, list)
    count = len(outs) if many else 1
    kinds = [ANY if far is True or i < far else VMEM for i in range(count)]
    return pl.pallas_call(
        kernel,
        out_shape=outs,
        in_specs=[SMEM] * scalars + [ANY] * anys + [VMEM] * (len(args) - scalars - anys),
        out_specs=kinds if many else kinds[0],
        scratch_shapes=list(scratch),
        compiler_params=pltpu.CompilerParams(vmem_limit_bytes=int(mib * 1024 * 1024)),
        cost_estimate=pl.CostEstimate(flops=10**8, bytes_accessed=4 * 10**6, transcendentals=0),
    )(*args)


def shape(*dims, dtype=BF):
    return jax.ShapeDtypeStruct(dims, dtype)


def shards(hidden, w_qkv, w_out, w_gate, w_up, w_down, g_attn, g_ffn, lengths, k_cache, v_cache):
    y, x = lax.axis_index("y"), lax.axis_index("x")
    place = (4 * y + x).astype(jnp.int32).reshape(1)
    hidden_t = hidden.T

    def swap(blocks):
        return lax.all_to_all(blocks, ("y", "x"), 0, 0)

    k_tall, v_tall = k_cache.transpose(0, 2, 1), v_cache.transpose(0, 2, 1)
    all_hidden = swap(
        call(
            start_kernel,
            shape(WID, OWN, WIDE),
            hidden_t,
            k_tall,
            v_tall,
            anys=3,
            far=True,
            mib=62,
            scratch=(
                pltpu.VMEM((OWN, ROWS), BF),
                pltpu.VMEM((2 * KVW, 128), BF),
                pltpu.VMEM((WID, OWN, WIDE), BF),
                pltpu.SemaphoreType.DMA((3 + WID,)),
            ),
        )
    ).reshape(D, WIDE)
    first = lax.all_gather(
        lax.all_gather(
            call(first_kernel, shape(w_qkv.shape[0], 128), w_qkv), "core", axis=0, tiled=True
        ),
        "z",
        axis=0,
        tiled=True,
    )
    second = lax.all_gather(
        call(second_kernel, shape(w_gate.shape[0], 896), w_gate, w_up, w_down.T, w_out),
        ("z", "core"),
        axis=0,
        tiled=True,
    )
    gate_up = jnp.concatenate([second[:, :FF_OWN], second[:, 256 : 256 + FF_OWN]], axis=1).T
    down = second[:, 512 : 512 + FF_OWN]
    sent = call(
        project_kernel,
        shape(WID, QKV_SEND, 128),
        place,
        all_hidden,
        first,
        g_attn.reshape(10, 128),
        scalars=1,
        far=True,
        scratch=(pltpu.VMEM((WID, QKV_SEND, 128), BF), pltpu.SemaphoreType.DMA((1,))),
    )
    mixed = swap(sent)
    places = jnp.concatenate([lengths[0] + jnp.arange(STRETCH), lengths[1:]]).astype(F32)
    ladder = jnp.arange(HALF).astype(F32) * (2.0 / HEAD_DIM)
    freqs = jnp.power(10000.0, -ladder)
    angles = freqs[:, None] * places[None, :STRETCH]
    flat = places[STRETCH:, None] * jnp.concatenate([freqs] * 4)[None, :]
    decodes, fresh_decode = call(
        decode_kernel,
        [shape(WID, 96, 128), shape(40, 128, dtype=F32)],
        lengths,
        place,
        k_tall,
        v_tall,
        mixed,
        jnp.concatenate([jnp.cos(flat), jnp.sin(flat)], axis=0),
        scalars=2,
        anys=2,
        far=True,
        mib=60,
        scratch=(
            pltpu.VMEM((2, 96, 128), BF),
            pltpu.VMEM((2 * KVW, 128), F32),
            pltpu.VMEM((GROUPS, 128, KVW), F32),
            pltpu.VMEM((GROUPS, 128, 128), F32),
            pltpu.VMEM((GROUPS, 128, KVW), F32),
            pltpu.VMEM((DECODES, KVW, SPAN), BF),
            pltpu.VMEM((DECODES, KVW, SPAN), BF),
            pltpu.SemaphoreType.DMA((2, WID + 1)),
        ),
    )
    decodes = swap(decodes)
    parts = call(
        prefill_kernel,
        shape(4, BLOCK, 128),
        lengths,
        place,
        mixed,
        jnp.cos(angles),
        jnp.sin(angles),
        scalars=2,
        far=True,
        scratch=(
            pltpu.VMEM((WID * QKV_OWN, 128), F32),
            pltpu.VMEM((2 * KVW, 128), F32),
            pltpu.VMEM((KV_HEADS, KEYS, HEAD_DIM), BF),
            pltpu.VMEM((KVW, KEYS), BF),
            pltpu.VMEM((KEYS, 128), F32),
            pltpu.VMEM((4 * HEADS, 128), F32),
            pltpu.VMEM((TAIL, 128), BF),
            pltpu.VMEM((4, BLOCK - TAIL, 128), BF),
            pltpu.SemaphoreType.DMA((8,)),
        ),
    )
    own_hidden = lax.dynamic_slice(all_hidden, (FEATS * y, 128 * x), (FEATS, 128))
    own_decode = lax.dynamic_slice(all_hidden, (FEATS * y, STRETCH), (FEATS, DECODES))
    out_own = lax.all_gather(
        call(
            tall_kernel,
            shape(OWN, D),
            parts,
            second,
            anys=2,
            mib=61,
            scratch=(pltpu.VMEM((D, 128), BF), pltpu.SemaphoreType.DMA((1,))),
        ),
        "x",
        axis=0,
        tiled=True,
    )
    middle, fresh_own = call(
        merge_kernel,
        [shape(WID, SEND, 128), shape(40, STRETCH, dtype=F32)],
        place,
        lax.all_to_all(parts, "y", 0, 0),
        decodes,
        out_own,
        own_hidden,
        own_decode,
        scalars=1,
        far=True,
        scratch=(
            pltpu.VMEM((D, 128), BF),
            pltpu.VMEM((SEND, 128), BF),
            pltpu.VMEM((40, STRETCH), F32),
            pltpu.SemaphoreType.DMA((WID + 1,)),
        ),
    )
    new_kv = jnp.concatenate([fresh_own, fresh_decode[:, :DECODES]], axis=1).astype(BF).T
    sums, residual = call(
        ffn_kernel,
        [shape(WID, OWN, ROWS), shape(OWN, ROWS)],
        place,
        gate_up,
        down,
        swap(middle),
        g_ffn.reshape(10, 128),
        scalars=1,
        anys=2,
        far=1,
        mib=24,
        scratch=(
            pltpu.VMEM((D, ROWS), BF),
            pltpu.VMEM((2 * FF_OWN, D), BF),
            pltpu.VMEM((D, FF_OWN), BF),
            pltpu.VMEM((WID, OWN, ROWS), BF),
            pltpu.SemaphoreType.DMA((6,)),
        ),
    )
    output = call(final_kernel, shape(OWN, ROWS), swap(sums), residual)
    return (output.T, new_kv)


def solution(mesh):
    core = 2 if mesh.shape["tok"] % 2 == 0 else 1
    devices = mesh.devices.reshape(mesh.shape["tok"] // core, core, 4, 4)
    finer = jax.sharding.Mesh(devices, ("z", "core", "y", "x"))
    tok, wid = ("z", "core"), ("y", "x")
    placed = (
        P(tok, wid),
        P(tok, wid),
        P(tok, wid),
        P(tok, wid),
        P(tok, wid),
        P(wid, tok),
        P(),
        P(),
        P(tok),
        P(tok, wid, None),
        P(tok, wid, None),
    )
    return jax.shard_map(
        shards,
        mesh=finer,
        in_specs=placed,
        out_specs=(P(tok, wid), P(tok, wid)),
        check_vma=False,
    )
```

```python
import jax
import jax.numpy as jnp
from jax import lax
from jax.experimental import pallas as pl
from jax.experimental.pallas import tpu as pltpu
from jax.sharding import PartitionSpec as P

D = 1280
HEADS = 20
KV_HEADS = 5
GROUPS = 4
HEAD_DIM = 64
HALF = 32
STRETCH = 512
DECODES = 16
ROWS = 528
SPAN = 128
WID = 16
QKV_OWN = 120
OWN = 80
FF_OWN = 224
KVW = 320
OLD = 4 * SPAN
KEYS = OLD + STRETCH // 4
FEATS = 320
BLOCK = 1408
TAIL = 1360
SEND = 352
QKV_SEND = 304
WIDE = 640
PIECE = 40

EPSILON = 1e-05
MASKED = -(2.0**100)
SCALE = 0.125
BF = jnp.bfloat16
F32 = jnp.float32


def dot(a, b, ca, cb):
    return lax.dot_general(a, b, (((ca,), (cb,)), ((), ())), preferred_element_type=F32)


def iota(shape, axis):
    return lax.broadcasted_iota(jnp.int32, shape, axis)


def split(x):
    high = x.astype(BF)
    return high, (x - high.astype(F32)).astype(BF)


def column(gain):
    square = jnp.concatenate([gain, jnp.zeros((118, 128), F32)], axis=0).T
    return jnp.concatenate([square[:, i : i + 1] for i in range(10)], axis=0)


def norm_cols(tall, gain):
    wide = tall.astype(F32)
    mean_square = jnp.sum(wide * wide, axis=0, keepdims=True) * (1.0 / D)
    return (wide * lax.rsqrt(mean_square + EPSILON) * gain).astype(BF)


def ship(pairs, sems):
    moves = [pltpu.make_async_copy(a, b, sems.at[i]) for i, (a, b) in enumerate(pairs)]
    for move in moves:
        move.start()
    for move in moves:
        move.wait()


def start_kernel(hidden_far, k_far, v_far, far, hidden, cache, out, sems):
    ship(
        [
            (hidden_far, hidden),
            (k_far.at[0], cache.at[pl.ds(0, KVW)]),
            (v_far.at[0], cache.at[pl.ds(KVW, KVW)]),
        ],
        sems,
    )
    main = hidden[:, 0:STRETCH]
    ending = hidden[:, STRETCH:ROWS].astype(F32)
    wide = cache[...].astype(F32)
    pad = jnp.zeros((OWN, 128 - DECODES - HEAD_DIM), F32)
    moves = []
    for i in range(WID):
        piece = wide[PIECE * i : PIECE * (i + 1)]
        halves = jnp.concatenate([piece[:, :HEAD_DIM], piece[:, HEAD_DIM:]], axis=0)
        out[i, :, 0:STRETCH] = main
        out[i, :, STRETCH:WIDE] = jnp.concatenate([ending, halves, pad], axis=1).astype(BF)
        moves.append(pltpu.make_async_copy(out.at[i], far.at[i], sems.at[3 + i]))
        moves[i].start()
    for move in moves:
        move.wait()


def first_kernel(qkv, out):
    out[...] = jnp.concatenate(
        [qkv[...].astype(F32), jnp.zeros((out.shape[0], 8), F32)], axis=1
    ).astype(BF)


def second_kernel(gate_far, up_far, down_far, projection_far, out, gate, up, down, projection, sems):
    ship(
        [(gate_far, gate), (up_far, up), (down_far, down), (projection_far, projection)],
        sems,
    )
    for i, ref in enumerate((gate, up, down)):
        out[:, 256 * i : 256 * (i + 1)] = jnp.concatenate(
            [ref[...].astype(F32), jnp.zeros((out.shape[0], 32), F32)], axis=1
        ).astype(BF)
    out[:, 768:896] = jnp.concatenate(
        [projection[...].astype(F32), jnp.zeros((out.shape[0], 48), F32)], axis=1
    ).astype(BF)


def tall_kernel(early, far, out, weight, sems):
    ship([(far.at[:, pl.ds(768, 128)], weight)], sems)
    out[...] = weight[...].astype(F32).T[:OWN].astype(BF)


def project_kernel(place, hidden, weight, gain, far, out, sems):
    w = place[0]
    normed = norm_cols(hidden[:, 0:ROWS], column(gain[...]))
    own = dot(weight[...], normed, 0, 0)
    same = (iota((128, 128), 0) == iota((128, 128), 1)).astype(BF)
    decoding = dot(own[:, STRETCH:ROWS].astype(BF), same, 0, 0).astype(BF)
    is_query = w * QKV_OWN + iota((128, 128), 0) < D
    for y in range(4):
        pieces = []
        for x in range(4):
            i = 4 * y + x
            ending = hidden[OWN * i : OWN * (i + 1), STRETCH:WIDE].astype(F32)
            ending = ending[:, DECODES : DECODES + HEAD_DIM]
            pieces.append(jnp.concatenate([ending[:PIECE], ending[PIECE:]], axis=1))
        caches = jnp.concatenate(pieces, axis=0).astype(BF)
        for x in range(4):
            block = jnp.where(
                is_query, own[:, 128 * x : 128 * (x + 1)], own[:, 128 * y : 128 * (y + 1)]
            )
            out[4 * y + x, 0:128, :] = block.astype(BF)
            out[4 * y + x, 128:144, :] = decoding
            out[4 * y + x, 144:QKV_SEND, :] = caches
    ship([(out, far)], sems)


def turn(x, cosine, sine):
    first, second = x[:HALF], x[HALF:]
    return jnp.concatenate(
        [first * cosine - second * sine, second * cosine + first * sine], axis=0
    )


def decode_kernel(lens, place, k_far, v_far, mixed, waves, far, fresh_far, out, fresh, qb, sc, od, k_cache, v_cache, sems):
    w = place[0]
    k_move = pltpu.make_async_copy(k_far.at[pl.ds(1, DECODES)], k_cache, sems.at[0, 0])
    v_move = pltpu.make_async_copy(v_far.at[pl.ds(1, DECODES)], v_cache, sems.at[0, 1])
    k_move.start()
    v_move.start()
    rows = jnp.concatenate(
        [mixed[i, 128:144, :].astype(F32)[:, :QKV_OWN] for i in range(WID)], axis=1
    )
    turned = rows[:, : D + KVW]
    ahead = pltpu.roll(turned, D + KVW - HALF, 1)
    behind = pltpu.roll(turned, HALF, 1)
    lane = iota((DECODES, D + KVW), 1) % HEAD_DIM
    cosine = jnp.concatenate([waves[0:DECODES, :]] * 13, axis=1)[:, : D + KVW]
    sine = jnp.concatenate([waves[DECODES : 2 * DECODES, :]] * 13, axis=1)[:, : D + KVW]
    turned = turned * cosine + jnp.where(lane < HALF, -ahead, behind) * sine
    turned = turned.astype(BF)
    both = jnp.concatenate([turned[:, D:].astype(F32), rows[:, D + KVW :]], axis=1).astype(BF)
    same = (iota((DECODES, 128), 0) == iota((DECODES, 128), 1)).astype(BF)
    fresh[...] = dot(both, same, 0, 0)
    pick = (iota((128, DECODES), 0) // 8 == iota((128, DECODES), 1)).astype(BF)
    place_g = (iota((8, KVW), 0) == iota((8, KVW), 1) // HEAD_DIM).astype(F32)
    grid_mask = jnp.broadcast_to(place_g[None], (DECODES, 8, KVW)).reshape(128, KVW)
    selves = dot(pick, both, 1, 0)
    k_self, v_self = selves[:, :KVW], selves[:, KVW:]
    own_row = iota((128, 1), 0) // 8 == w
    wide = turned.astype(F32)
    self_score = []
    for k in range(GROUPS):
        part = jnp.concatenate(
            [
                wide[:, HEAD_DIM * (GROUPS * g + k) : HEAD_DIM * (GROUPS * g + k + 1)]
                for g in range(KV_HEADS)
            ],
            axis=1,
        )
        query = dot(pick, part.astype(BF), 1, 0) * grid_mask * SCALE
        qb[k] = query
        self_score.append(
            jnp.where(own_row, jnp.sum(query * k_self, axis=1, keepdims=True), MASKED)
        )
    k_move.wait()
    for j in range(DECODES):
        query = jnp.concatenate([qb[k, 8 * j : 8 * j + 8, :] for k in range(GROUPS)], axis=0)
        score = dot(query.astype(BF), k_cache[j], 1, 0)
        spots = w * SPAN + iota((32, SPAN), 1)
        score = jnp.where(spots < lens[j + 1], score, MASKED)
        for k in range(GROUPS):
            sc[k, 8 * j : 8 * j + 8, :] = score[8 * k : 8 * k + 8]
    lane = iota((128, 128), 1)
    group = iota((128, 128), 0) % 8
    table = jnp.zeros((128, 128), F32)
    self_weight = []
    for k in range(GROUPS):
        head = jnp.where(group < KV_HEADS, GROUPS * group + k, 1000)
        score = sc[k]
        top, low = split(jnp.maximum(jnp.max(score, axis=1, keepdims=True), self_score[k]))
        top, low = top.astype(F32), low.astype(F32)
        expo = jnp.exp(score - (top + low))
        own = jnp.exp(self_score[k] - (top + low))
        total, rest = split(jnp.sum(expo, axis=1, keepdims=True) + own)
        sc[k] = expo
        self_weight.append(own)
        for i, part in enumerate((top, low, total.astype(F32), rest.astype(F32))):
            table = jnp.where(lane == HEADS * i + head, part, table)
    v_move.wait()
    for j in range(DECODES):
        expo = jnp.concatenate([sc[k, 8 * j : 8 * j + 8, :] for k in range(GROUPS)], axis=0)
        summed = dot(expo.astype(BF), v_cache[j], 1, 1)
        for k in range(GROUPS):
            od[k, 8 * j : 8 * j + 8, :] = summed[8 * k : 8 * k + 8]
    marks = dot(pick, table.astype(BF), 0, 0)
    flat = []
    for k in range(GROUPS):
        part = ((od[k] + self_weight[k] * v_self) * grid_mask).astype(BF)
        flat.append(dot(pick, part, 0, 0))
    decoded = jnp.concatenate(
        [flat[h % GROUPS][:, HEAD_DIM * (h // GROUPS) :][:, :HEAD_DIM] for h in range(HEADS)], axis=1
    )
    for half in range(2):
        rows = slice(8 * half, 8 * half + 8)
        block = jnp.concatenate(
            [decoded[rows, 128 * t : 128 * (t + 1)] for t in range(10)]
            + [marks[rows], jnp.zeros((8, 128), F32)],
            axis=0,
        ).astype(BF)
        out[half] = block
    at = pl.multiple_of(40 * w, 8)
    ship(
        [(out.at[i % 4 // 2], far.at[i]) for i in range(WID)] + [(fresh.at[pl.ds(at, 40)], fresh_far)],
        sems.at[1],
    )


def prefill_kernel(lens, place, mixed, cosine, sine, far, tall, fresh, keys, vals, bias, stats, parts, tails, sems):
    w = place[0]
    y, x = w // 4, w % 4
    for i in range(WID):
        tall[QKV_OWN * i : QKV_OWN * (i + 1), :] = mixed[i, 0:128, :].astype(F32)[:QKV_OWN]
    old = [mixed[i, 144:QKV_SEND, :].astype(F32) for i in range(WID)]
    caches = [
        jnp.concatenate([o[PIECE * i : PIECE * (i + 1)] for o in old], axis=0) for i in range(4)
    ]
    cols_x = pl.ds(pl.multiple_of(x * 128, 128), 128)
    cols_y = pl.ds(pl.multiple_of(y * 128, 128), 128)
    cos_x, sin_x, cos_y, sin_y = cosine[:, cols_x], sine[:, cols_x], cosine[:, cols_y], sine[:, cols_y]
    for g in range(KV_HEADS):
        rows = slice(HEAD_DIM * g, HEAD_DIM * (g + 1))
        turned = turn(tall[D + HEAD_DIM * g : D + HEAD_DIM * (g + 1), :], cos_y, sin_y).astype(BF)
        fresh[rows, :] = turned.astype(F32)
        keys[g, OLD:KEYS, :] = turned.astype(F32).T.astype(BF)
        for i in range(4):
            keys[g, 128 * i : 128 * (i + 1), :] = caches[i][rows].T.astype(BF)
    fresh[KVW:, :] = tall[D + KVW :, :]
    for i in range(4):
        vals[:, 128 * i : 128 * (i + 1)] = caches[i][KVW:].astype(BF)
    vals[:, OLD:KEYS] = tall[D + KVW :, :].astype(BF)
    spots = y * OLD + iota((OLD, 128), 0)
    bias[0:OLD, :] = jnp.where(spots < lens[0], 0.0, MASKED)
    later = x * 128 + iota((128, 128), 1)
    earlier = y * 128 + iota((128, 128), 0)
    bias[OLD:KEYS, :] = jnp.where(earlier <= later, 0.0, MASKED)
    for g in range(KV_HEADS):
        queries = []
        for k in range(GROUPS):
            at = HEAD_DIM * (GROUPS * g + k)
            query = turn(tall[at : at + HEAD_DIM, :], cos_x, sin_x)
            queries.append((query.astype(BF).astype(F32) * SCALE).astype(BF))
        scores = dot(keys[g], jnp.concatenate(queries, axis=1), 1, 0)
        expos = []
        for k in range(GROUPS):
            h = GROUPS * g + k
            score = scores[:, 128 * k : 128 * (k + 1)] + bias[...]
            top, low = split(jnp.max(score, axis=0, keepdims=True))
            top, low = top.astype(F32), low.astype(F32)
            expo = jnp.exp(score - (top + low))
            total, rest = split(jnp.sum(expo, axis=0, keepdims=True))
            for i, part in enumerate((top, low, total.astype(F32), rest.astype(F32))):
                stats[HEADS * i + h : HEADS * i + h + 1, :] = part
            expos.append(expo.astype(BF))
        summed = dot(
            vals[HEAD_DIM * g : HEAD_DIM * (g + 1), :], jnp.concatenate(expos, axis=1), 1, 0
        ).astype(BF)
        for k in range(GROUPS):
            h = GROUPS * g + k
            parts[HEAD_DIM * h : HEAD_DIM * (h + 1), :] = summed[:, 128 * k : 128 * (k + 1)]
    parts[D:TAIL, :] = stats[...].astype(BF)
    for i in range(4):
        at = pl.multiple_of(40 * (4 * i + x), 8)
        tails[i] = jnp.concatenate([fresh[pl.ds(at, 40), :], jnp.zeros((8, 128), F32)], axis=0).astype(BF)
    ship(
        [(parts, far.at[i, pl.ds(0, TAIL)]) for i in range(4)]
        + [(tails.at[i], far.at[i, pl.ds(TAIL, BLOCK - TAIL)]) for i in range(4)],
        sems,
    )


def merge_shares(peaks, totals):
    peak = peaks[0]
    for p in peaks[1:]:
        peak = jnp.maximum(peak, p)
    shares = [jnp.exp(p - peak) for p in peaks]
    whole = shares[0] * totals[0]
    for share, total in zip(shares[1:], totals[1:]):
        whole = whole + share * total
    inverse = 1.0 / whole
    return [share * inverse for share in shares]


def tiles(rows):
    wide = jnp.concatenate([rows, jnp.zeros((8, 384 - FEATS), F32)], axis=1)
    return [wide[:, 128 * t : 128 * (t + 1)] for t in range(3)]


def rows_of(blocks, index):
    tail = blocks[index].astype(F32)
    return [tail[0:8], tail[8:16], tail[16:24, :HEAD_DIM]]


def merge_kernel(
    place, parts_far, decodes, weight, hidden, hidden_dec, far, fresh_far, tall, out, fresh, parts, sems, land
):
    x = place[0] % 4
    lands = []
    for i in range(5):
        rows = pl.ds(FEATS * i, FEATS if i < 4 else BLOCK - D)
        lands.append(pltpu.make_async_copy(parts_far.at[:, rows], parts.at[:, rows], land.at[i]))
    for i in (4, 0, 1, 2, 3):
        lands[i].start()
    near = [decodes[s].astype(F32) for s in range(WID)]
    marks = [n[80:88] for n in near]
    shares = merge_shares(
        [m[:, 0:20] + m[:, 20:40] for m in marks], [m[:, 40:60] + m[:, 60:80] for m in marks]
    )
    low = iota((8, 128), 1) < HEAD_DIM
    decoded = [jnp.zeros((8, 128), F32) for t in range(10)]
    for s in range(WID):
        for t in range(10):
            share = jnp.where(low, shares[s][:, 2 * t : 2 * t + 1], shares[s][:, 2 * t + 1 : 2 * t + 2])
            decoded[t] = decoded[t] + share * near[s][8 * t : 8 * t + 8]
    rows = jnp.concatenate(decoded, axis=1).astype(BF)
    pick = (iota((8, DECODES), 1) == x // 2 * 8 + iota((8, DECODES), 0)).astype(BF)
    own_rows = dot(pick, hidden_dec[...], 1, 1) + dot(rows, weight[...], 1, 1)
    tail = jnp.concatenate(tiles(own_rows) + [jnp.zeros((8, 128), F32)], axis=0).astype(BF)
    lands[4].wait()
    extra = [parts[s, D:BLOCK, :].astype(F32) for s in range(4)]
    shares = merge_shares(
        [m[0:20] + m[20:40] for m in extra], [m[40:60] + m[60:80] for m in extra]
    )
    for s in range(4):
        fresh[:, 128 * s : 128 * (s + 1)] = extra[s][80:120]
    for h in range(HEADS):
        if h % 5 == 0:
            lands[h // 5].wait()
        rows = slice(HEAD_DIM * h, HEAD_DIM * (h + 1))
        total = shares[0][h : h + 1] * parts[0, rows, :].astype(F32)
        for s in range(1, 4):
            total = total + shares[s][h : h + 1] * parts[s, rows, :].astype(F32)
        tall[rows, :] = total.astype(BF)
    own = hidden[...].astype(F32) + dot(weight[...], tall[...], 1, 0)
    out[0:FEATS, :] = own.astype(BF)
    out[FEATS:SEND, :] = tail
    ship([(out, far.at[i]) for i in range(WID)] + [(fresh, fresh_far)], sems)


def ffn_kernel(
    place, far_weight, far_down, blocks, gain, far, residual, middle, weight, down, out, tails, sems, land
):
    w = place[0]
    weight_move = pltpu.make_async_copy(far_weight, weight, sems.at[0])
    down_move = pltpu.make_async_copy(far_down, down, sems.at[1])
    lands = [pltpu.make_async_copy(blocks.at[:, pl.ds(FEATS, SEND - FEATS)], tails, land.at[WID])]
    for y in range(4):
        for x in range(4):
            lands.append(
                pltpu.make_async_copy(
                    blocks.at[4 * y + x, pl.ds(0, FEATS)],
                    middle.at[pl.ds(FEATS * y, FEATS), pl.ds(128 * x, 128)],
                    land.at[4 * y + x],
                )
            )
    for move in lands:
        move.start()
    weight_move.start()
    down_move.start()
    lands[0].wait()
    rows = jnp.concatenate(
        [
            jnp.concatenate([t for y in range(4) for t in rows_of(tails, 4 * y + x)], axis=1)
            for x in (0, 2)
        ],
        axis=0,
    )
    same = (iota((DECODES, DECODES), 0) == iota((DECODES, DECODES), 1)).astype(BF)
    for move in lands[1:]:
        move.wait()
    middle[:, STRETCH:ROWS] = dot(rows.astype(BF), same, 0, 0).astype(BF)
    residual[...] = middle[pl.ds(pl.multiple_of(w * OWN, OWN), OWN), :]
    normed = norm_cols(middle[...], column(gain[...]))
    weight_move.wait()
    both = dot(weight[...], normed, 1, 0)
    gate, up = both[:FF_OWN], both[FF_OWN:]
    act = (gate / (1.0 + jnp.exp(-gate)) * up).astype(BF)
    down_move.wait()
    moves = []
    for i in range(4):
        part = dot(down[FEATS * i : FEATS * (i + 1), :], act, 1, 0).astype(BF)
        for j in range(4):
            out[4 * i + j] = part[OWN * j : OWN * (j + 1)]
        rows = pl.ds(4 * i, 4)
        moves.append(pltpu.make_async_copy(out.at[rows], far.at[rows], sems.at[2 + i]))
        moves[i].start()
    for move in moves:
        move.wait()


def final_kernel(parts, residual, out):
    total = residual[...].astype(F32)
    for s in range(WID):
        total = total + parts[s].astype(F32)
    out[...] = total.astype(BF)


VMEM = pl.BlockSpec(memory_space=pltpu.VMEM)
SMEM = pl.BlockSpec(memory_space=pltpu.SMEM)
ANY = pl.BlockSpec(memory_space=pltpu.HBM)


def call(kernel, outs, *args, scalars=0, anys=0, scratch=(), mib=16, far=False):
    many = isinstance(outs, list)
    count = len(outs) if many else 1
    kinds = [ANY if far is True or i < far else VMEM for i in range(count)]
    return pl.pallas_call(
        kernel,
        out_shape=outs,
        in_specs=[SMEM] * scalars + [ANY] * anys + [VMEM] * (len(args) - scalars - anys),
        out_specs=kinds if many else kinds[0],
        scratch_shapes=list(scratch),
        compiler_params=pltpu.CompilerParams(vmem_limit_bytes=int(mib * 1024 * 1024)),
        cost_estimate=pl.CostEstimate(flops=10**8, bytes_accessed=4 * 10**6, transcendentals=0),
    )(*args)


def shape(*dims, dtype=BF):
    return jax.ShapeDtypeStruct(dims, dtype)


def shards(hidden, w_qkv, w_out, w_gate, w_up, w_down, g_attn, g_ffn, lengths, k_cache, v_cache):
    y, x = lax.axis_index("y"), lax.axis_index("x")
    place = (4 * y + x).astype(jnp.int32).reshape(1)
    hidden_t = hidden.T

    def swap(blocks):
        return lax.all_to_all(blocks, ("y", "x"), 0, 0)

    k_tall, v_tall = k_cache.transpose(0, 2, 1), v_cache.transpose(0, 2, 1)
    all_hidden = swap(
        call(
            start_kernel,
            shape(WID, OWN, WIDE),
            hidden_t,
            k_tall,
            v_tall,
            anys=3,
            far=True,
            mib=62,
            scratch=(
                pltpu.VMEM((OWN, ROWS), BF),
                pltpu.VMEM((2 * KVW, 128), BF),
                pltpu.VMEM((WID, OWN, WIDE), BF),
                pltpu.SemaphoreType.DMA((3 + WID,)),
            ),
        )
    ).reshape(D, WIDE)
    first = lax.all_gather(
        lax.all_gather(
            call(first_kernel, shape(w_qkv.shape[0], 128), w_qkv), "core", axis=0, tiled=True
        ),
        "z",
        axis=0,
        tiled=True,
    )
    second = lax.all_gather(
        call(
            second_kernel,
            shape(w_gate.shape[0], 896),
            w_gate,
            w_up,
            w_down.T,
            w_out,
            anys=4,
            mib=62,
            scratch=(
                pltpu.VMEM(w_gate.shape, BF),
                pltpu.VMEM(w_up.shape, BF),
                pltpu.VMEM(w_down.shape[::-1], BF),
                pltpu.VMEM(w_out.shape, BF),
                pltpu.SemaphoreType.DMA((4,)),
            ),
        ),
        ("z", "core"),
        axis=0,
        tiled=True,
    )
    gate_up = jnp.concatenate([second[:, :FF_OWN], second[:, 256 : 256 + FF_OWN]], axis=1).T
    down = second[:, 512 : 512 + FF_OWN]
    sent = call(
        project_kernel,
        shape(WID, QKV_SEND, 128),
        place,
        all_hidden,
        first,
        g_attn.reshape(10, 128),
        scalars=1,
        far=True,
        scratch=(pltpu.VMEM((WID, QKV_SEND, 128), BF), pltpu.SemaphoreType.DMA((1,))),
    )
    mixed = swap(sent)
    places = jnp.concatenate([lengths[0] + jnp.arange(STRETCH), lengths[1:]]).astype(F32)
    ladder = jnp.arange(HALF).astype(F32) * (2.0 / HEAD_DIM)
    freqs = jnp.power(10000.0, -ladder)
    angles = freqs[:, None] * places[None, :STRETCH]
    flat = places[STRETCH:, None] * jnp.concatenate([freqs] * 4)[None, :]
    decodes, fresh_decode = call(
        decode_kernel,
        [shape(WID, 96, 128), shape(40, 128, dtype=F32)],
        lengths,
        place,
        k_tall,
        v_tall,
        mixed,
        jnp.concatenate([jnp.cos(flat), jnp.sin(flat)], axis=0),
        scalars=2,
        anys=2,
        far=True,
        mib=60,
        scratch=(
            pltpu.VMEM((2, 96, 128), BF),
            pltpu.VMEM((2 * KVW, 128), F32),
            pltpu.VMEM((GROUPS, 128, KVW), F32),
            pltpu.VMEM((GROUPS, 128, 128), F32),
            pltpu.VMEM((GROUPS, 128, KVW), F32),
            pltpu.VMEM((DECODES, KVW, SPAN), BF),
            pltpu.VMEM((DECODES, KVW, SPAN), BF),
            pltpu.SemaphoreType.DMA((2, WID + 1)),
        ),
    )
    decodes = swap(decodes)
    parts = call(
        prefill_kernel,
        shape(4, BLOCK, 128),
        lengths,
        place,
        mixed,
        jnp.cos(angles),
        jnp.sin(angles),
        scalars=2,
        far=True,
        scratch=(
            pltpu.VMEM((WID * QKV_OWN, 128), F32),
            pltpu.VMEM((2 * KVW, 128), F32),
            pltpu.VMEM((KV_HEADS, KEYS, HEAD_DIM), BF),
            pltpu.VMEM((KVW, KEYS), BF),
            pltpu.VMEM((KEYS, 128), F32),
            pltpu.VMEM((4 * HEADS, 128), F32),
            pltpu.VMEM((TAIL, 128), BF),
            pltpu.VMEM((4, BLOCK - TAIL, 128), BF),
            pltpu.SemaphoreType.DMA((8,)),
        ),
    )
    own_hidden = lax.dynamic_slice(all_hidden, (FEATS * y, 128 * x), (FEATS, 128))
    own_decode = lax.dynamic_slice(all_hidden, (FEATS * y, STRETCH), (FEATS, DECODES))
    out_own = lax.all_gather(
        call(
            tall_kernel,
            shape(OWN, D),
            parts,
            second,
            anys=2,
            mib=61,
            scratch=(pltpu.VMEM((D, 128), BF), pltpu.SemaphoreType.DMA((1,))),
        ),
        "x",
        axis=0,
        tiled=True,
    )
    middle, fresh_own = call(
        merge_kernel,
        [shape(WID, SEND, 128), shape(40, STRETCH, dtype=F32)],
        place,
        lax.all_to_all(parts, "y", 0, 0),
        decodes,
        out_own,
        own_hidden,
        own_decode,
        scalars=1,
        anys=1,
        far=True,
        scratch=(
            pltpu.VMEM((D, 128), BF),
            pltpu.VMEM((SEND, 128), BF),
            pltpu.VMEM((40, STRETCH), F32),
            pltpu.VMEM((4, BLOCK, 128), BF),
            pltpu.SemaphoreType.DMA((WID + 1,)),
            pltpu.SemaphoreType.DMA((5,)),
        ),
    )
    new_kv = jnp.concatenate([fresh_own, fresh_decode[:, :DECODES]], axis=1).astype(BF).T
    sums, residual = call(
        ffn_kernel,
        [shape(WID, OWN, ROWS), shape(OWN, ROWS)],
        place,
        gate_up,
        down,
        swap(middle),
        g_ffn.reshape(10, 128),
        scalars=1,
        anys=3,
        far=1,
        mib=58,
        scratch=(
            pltpu.VMEM((D, ROWS), BF),
            pltpu.VMEM((2 * FF_OWN, D), BF),
            pltpu.VMEM((D, FF_OWN), BF),
            pltpu.VMEM((WID, OWN, ROWS), BF),
            pltpu.VMEM((WID, SEND - FEATS, 128), BF),
            pltpu.SemaphoreType.DMA((6,)),
            pltpu.SemaphoreType.DMA((WID + 1,)),
        ),
    )
    output = call(final_kernel, shape(OWN, ROWS), swap(sums), residual)
    return (output.T, new_kv)


def solution(mesh):
    core = 2 if mesh.shape["tok"] % 2 == 0 else 1
    devices = mesh.devices.reshape(mesh.shape["tok"] // core, core, 4, 4)
    finer = jax.sharding.Mesh(devices, ("z", "core", "y", "x"))
    tok, wid = ("z", "core"), ("y", "x")
    placed = (
        P(tok, wid),
        P(tok, wid),
        P(tok, wid),
        P(tok, wid),
        P(tok, wid),
        P(wid, tok),
        P(),
        P(),
        P(tok),
        P(tok, wid, None),
        P(tok, wid, None),
    )
    return jax.shard_map(
        shards,
        mesh=finer,
        in_specs=placed,
        out_specs=(P(tok, wid), P(tok, wid)),
        check_vma=False,
    )
```

```python
import jax
import jax.numpy as jnp
from jax import lax
from jax.experimental import pallas as pl
from jax.experimental.pallas import tpu as pltpu
from jax.sharding import PartitionSpec as P

D = 1280
HEADS = 20
KV_HEADS = 5
GROUPS = 4
HEAD_DIM = 64
HALF = 32
STRETCH = 512
DECODES = 16
ROWS = 528
SPAN = 128
WID = 16
QKV_OWN = 120
OWN = 80
FF_OWN = 224
KVW = 320
OLD = 4 * SPAN
KEYS = OLD + STRETCH // 4
FEATS = 320
BLOCK = 1408
TAIL = 1360
SEND = 352
QKV_SEND = 304
WIDE = 640
PIECE = 40

EPSILON = 1e-05
MASKED = -(2.0**100)
SCALE = 0.125
BF = jnp.bfloat16
F32 = jnp.float32


def dot(a, b, ca, cb):
    return lax.dot_general(a, b, (((ca,), (cb,)), ((), ())), preferred_element_type=F32)


def iota(shape, axis):
    return lax.broadcasted_iota(jnp.int32, shape, axis)


def split(x):
    high = x.astype(BF)
    return high, (x - high.astype(F32)).astype(BF)


def column(gain):
    square = jnp.concatenate([gain, jnp.zeros((118, 128), F32)], axis=0).T
    return jnp.concatenate([square[:, i : i + 1] for i in range(10)], axis=0)


def norm_cols(tall, gain):
    wide = tall.astype(F32)
    mean_square = jnp.sum(wide * wide, axis=0, keepdims=True) * (1.0 / D)
    return (wide * lax.rsqrt(mean_square + EPSILON) * gain).astype(BF)


def ship(pairs, sems):
    moves = [pltpu.make_async_copy(a, b, sems.at[i]) for i, (a, b) in enumerate(pairs)]
    for move in moves:
        move.start()
    for move in moves:
        move.wait()


def start_kernel(hidden_far, k_far, v_far, far, hidden, cache, out, sems):
    ship(
        [
            (hidden_far, hidden),
            (k_far.at[0], cache.at[pl.ds(0, KVW)]),
            (v_far.at[0], cache.at[pl.ds(KVW, KVW)]),
        ],
        sems,
    )
    main = hidden[:, 0:STRETCH]
    ending = hidden[:, STRETCH:ROWS].astype(F32)
    wide = cache[...].astype(F32)
    pad = jnp.zeros((OWN, 128 - DECODES - HEAD_DIM), F32)
    moves = []
    for i in range(WID):
        piece = wide[PIECE * i : PIECE * (i + 1)]
        halves = jnp.concatenate([piece[:, :HEAD_DIM], piece[:, HEAD_DIM:]], axis=0)
        out[i, :, 0:STRETCH] = main
        out[i, :, STRETCH:WIDE] = jnp.concatenate([ending, halves, pad], axis=1).astype(BF)
        moves.append(pltpu.make_async_copy(out.at[i], far.at[i], sems.at[3 + i]))
        moves[i].start()
    for move in moves:
        move.wait()


def first_kernel(qkv, out):
    out[...] = jnp.concatenate(
        [qkv[...].astype(F32), jnp.zeros((out.shape[0], 8), F32)], axis=1
    ).astype(BF)


def second_kernel(gate_far, up_far, down_far, projection_far, out, gate, up, down, projection, sems):
    ship(
        [(gate_far, gate), (up_far, up), (down_far, down), (projection_far, projection)],
        sems,
    )
    for i, ref in enumerate((gate, up, down)):
        out[:, 256 * i : 256 * (i + 1)] = jnp.concatenate(
            [ref[...].astype(F32), jnp.zeros((out.shape[0], 32), F32)], axis=1
        ).astype(BF)
    out[:, 768:896] = jnp.concatenate(
        [projection[...].astype(F32), jnp.zeros((out.shape[0], 48), F32)], axis=1
    ).astype(BF)


def tall_kernel(early, far, out, weight, sems):
    ship([(far.at[:, pl.ds(768, 128)], weight)], sems)
    out[...] = weight[...].astype(F32).T[:OWN].astype(BF)


def project_kernel(place, hidden, weight, gain, far, out, sems):
    w = place[0]
    normed = norm_cols(hidden[:, 0:ROWS], column(gain[...]))
    own = dot(weight[...], normed, 0, 0)
    same = (iota((128, 128), 0) == iota((128, 128), 1)).astype(BF)
    decoding = dot(own[:, STRETCH:ROWS].astype(BF), same, 0, 0).astype(BF)
    is_query = w * QKV_OWN + iota((128, 128), 0) < D
    for y in range(4):
        pieces = []
        for x in range(4):
            i = 4 * y + x
            ending = hidden[OWN * i : OWN * (i + 1), STRETCH:WIDE].astype(F32)
            ending = ending[:, DECODES : DECODES + HEAD_DIM]
            pieces.append(jnp.concatenate([ending[:PIECE], ending[PIECE:]], axis=1))
        caches = jnp.concatenate(pieces, axis=0).astype(BF)
        for x in range(4):
            block = jnp.where(
                is_query, own[:, 128 * x : 128 * (x + 1)], own[:, 128 * y : 128 * (y + 1)]
            )
            out[4 * y + x, 0:128, :] = block.astype(BF)
            out[4 * y + x, 128:144, :] = decoding
            out[4 * y + x, 144:QKV_SEND, :] = caches
    ship([(out, far)], sems)


def turn(x, cosine, sine):
    first, second = x[:HALF], x[HALF:]
    return jnp.concatenate(
        [first * cosine - second * sine, second * cosine + first * sine], axis=0
    )


def decode_kernel(lens, place, k_far, v_far, mixed, waves, far, fresh_far, out, fresh, qb, sc, od, k_cache, v_cache, sems):
    w = place[0]
    k_move = pltpu.make_async_copy(k_far.at[pl.ds(1, DECODES)], k_cache, sems.at[0, 0])
    v_move = pltpu.make_async_copy(v_far.at[pl.ds(1, DECODES)], v_cache, sems.at[0, 1])
    k_move.start()
    v_move.start()
    rows = jnp.concatenate(
        [mixed[i, 128:144, :].astype(F32)[:, :QKV_OWN] for i in range(WID)], axis=1
    )
    turned = rows[:, : D + KVW]
    ahead = pltpu.roll(turned, D + KVW - HALF, 1)
    behind = pltpu.roll(turned, HALF, 1)
    lane = iota((DECODES, D + KVW), 1) % HEAD_DIM
    cosine = jnp.concatenate([waves[0:DECODES, :]] * 13, axis=1)[:, : D + KVW]
    sine = jnp.concatenate([waves[DECODES : 2 * DECODES, :]] * 13, axis=1)[:, : D + KVW]
    turned = turned * cosine + jnp.where(lane < HALF, -ahead, behind) * sine
    turned = turned.astype(BF)
    both = jnp.concatenate([turned[:, D:].astype(F32), rows[:, D + KVW :]], axis=1).astype(BF)
    same = (iota((DECODES, 128), 0) == iota((DECODES, 128), 1)).astype(BF)
    fresh[...] = dot(both, same, 0, 0)
    pick = (iota((128, DECODES), 0) // 8 == iota((128, DECODES), 1)).astype(BF)
    place_g = (iota((8, KVW), 0) == iota((8, KVW), 1) // HEAD_DIM).astype(F32)
    grid_mask = jnp.broadcast_to(place_g[None], (DECODES, 8, KVW)).reshape(128, KVW)
    selves = dot(pick, both, 1, 0)
    k_self, v_self = selves[:, :KVW], selves[:, KVW:]
    own_row = iota((128, 1), 0) // 8 == w
    wide = turned.astype(F32)
    self_score = []
    for k in range(GROUPS):
        part = jnp.concatenate(
            [
                wide[:, HEAD_DIM * (GROUPS * g + k) : HEAD_DIM * (GROUPS * g + k + 1)]
                for g in range(KV_HEADS)
            ],
            axis=1,
        )
        query = dot(pick, part.astype(BF), 1, 0) * grid_mask * SCALE
        qb[k] = query
        self_score.append(
            jnp.where(own_row, jnp.sum(query * k_self, axis=1, keepdims=True), MASKED)
        )
    k_move.wait()
    for j in range(DECODES):
        query = jnp.concatenate([qb[k, 8 * j : 8 * j + 8, :] for k in range(GROUPS)], axis=0)
        score = dot(query.astype(BF), k_cache[j], 1, 0)
        spots = w * SPAN + iota((32, SPAN), 1)
        score = jnp.where(spots < lens[j + 1], score, MASKED)
        for k in range(GROUPS):
            sc[k, 8 * j : 8 * j + 8, :] = score[8 * k : 8 * k + 8]
    lane = iota((128, 128), 1)
    group = iota((128, 128), 0) % 8
    table = jnp.zeros((128, 128), F32)
    self_weight = []
    for k in range(GROUPS):
        head = jnp.where(group < KV_HEADS, GROUPS * group + k, 1000)
        score = sc[k]
        top, low = split(jnp.maximum(jnp.max(score, axis=1, keepdims=True), self_score[k]))
        top, low = top.astype(F32), low.astype(F32)
        expo = jnp.exp(score - (top + low))
        own = jnp.exp(self_score[k] - (top + low))
        total, rest = split(jnp.sum(expo, axis=1, keepdims=True) + own)
        sc[k] = expo
        self_weight.append(own)
        for i, part in enumerate((top, low, total.astype(F32), rest.astype(F32))):
            table = jnp.where(lane == HEADS * i + head, part, table)
    v_move.wait()
    for j in range(DECODES):
        expo = jnp.concatenate([sc[k, 8 * j : 8 * j + 8, :] for k in range(GROUPS)], axis=0)
        summed = dot(expo.astype(BF), v_cache[j], 1, 1)
        for k in range(GROUPS):
            od[k, 8 * j : 8 * j + 8, :] = summed[8 * k : 8 * k + 8]
    marks = dot(pick, table.astype(BF), 0, 0)
    flat = []
    for k in range(GROUPS):
        part = ((od[k] + self_weight[k] * v_self) * grid_mask).astype(BF)
        flat.append(dot(pick, part, 0, 0))
    decoded = jnp.concatenate(
        [flat[h % GROUPS][:, HEAD_DIM * (h // GROUPS) :][:, :HEAD_DIM] for h in range(HEADS)], axis=1
    )
    for half in range(2):
        rows = slice(8 * half, 8 * half + 8)
        block = jnp.concatenate(
            [decoded[rows, 128 * t : 128 * (t + 1)] for t in range(10)]
            + [marks[rows], jnp.zeros((8, 128), F32)],
            axis=0,
        ).astype(BF)
        out[half] = block
    at = pl.multiple_of(40 * w, 8)
    ship(
        [(out.at[i % 4 // 2], far.at[i]) for i in range(WID)] + [(fresh.at[pl.ds(at, 40)], fresh_far)],
        sems.at[1],
    )


def prefill_kernel(lens, place, mixed, cosine, sine, far, tall, fresh, keys, vals, bias, stats, parts, tails, sems):
    w = place[0]
    y, x = w // 4, w % 4
    for i in range(WID):
        tall[QKV_OWN * i : QKV_OWN * (i + 1), :] = mixed[i, 0:128, :].astype(F32)[:QKV_OWN]
    old = [mixed[i, 144:QKV_SEND, :].astype(F32) for i in range(WID)]
    caches = [
        jnp.concatenate([o[PIECE * i : PIECE * (i + 1)] for o in old], axis=0) for i in range(4)
    ]
    cols_x = pl.ds(pl.multiple_of(x * 128, 128), 128)
    cols_y = pl.ds(pl.multiple_of(y * 128, 128), 128)
    cos_x, sin_x, cos_y, sin_y = cosine[:, cols_x], sine[:, cols_x], cosine[:, cols_y], sine[:, cols_y]
    for g in range(KV_HEADS):
        rows = slice(HEAD_DIM * g, HEAD_DIM * (g + 1))
        turned = turn(tall[D + HEAD_DIM * g : D + HEAD_DIM * (g + 1), :], cos_y, sin_y).astype(BF)
        fresh[rows, :] = turned.astype(F32)
        keys[g, OLD:KEYS, :] = turned.astype(F32).T.astype(BF)
        for i in range(4):
            keys[g, 128 * i : 128 * (i + 1), :] = caches[i][rows].T.astype(BF)
    fresh[KVW:, :] = tall[D + KVW :, :]
    for i in range(4):
        vals[:, 128 * i : 128 * (i + 1)] = caches[i][KVW:].astype(BF)
    vals[:, OLD:KEYS] = tall[D + KVW :, :].astype(BF)
    spots = y * OLD + iota((OLD, 128), 0)
    bias[0:OLD, :] = jnp.where(spots < lens[0], 0.0, MASKED)
    later = x * 128 + iota((128, 128), 1)
    earlier = y * 128 + iota((128, 128), 0)
    bias[OLD:KEYS, :] = jnp.where(earlier <= later, 0.0, MASKED)
    for g in range(KV_HEADS):
        queries = []
        for k in range(GROUPS):
            at = HEAD_DIM * (GROUPS * g + k)
            query = turn(tall[at : at + HEAD_DIM, :], cos_x, sin_x)
            queries.append((query.astype(BF).astype(F32) * SCALE).astype(BF))
        scores = dot(keys[g], jnp.concatenate(queries, axis=1), 1, 0)
        expos = []
        for k in range(GROUPS):
            h = GROUPS * g + k
            score = scores[:, 128 * k : 128 * (k + 1)] + bias[...]
            top, low = split(jnp.max(score, axis=0, keepdims=True))
            top, low = top.astype(F32), low.astype(F32)
            expo = jnp.exp(score - (top + low))
            total, rest = split(jnp.sum(expo, axis=0, keepdims=True))
            for i, part in enumerate((top, low, total.astype(F32), rest.astype(F32))):
                stats[HEADS * i + h : HEADS * i + h + 1, :] = part
            expos.append(expo.astype(BF))
        summed = dot(
            vals[HEAD_DIM * g : HEAD_DIM * (g + 1), :], jnp.concatenate(expos, axis=1), 1, 0
        ).astype(BF)
        for k in range(GROUPS):
            h = GROUPS * g + k
            parts[HEAD_DIM * h : HEAD_DIM * (h + 1), :] = summed[:, 128 * k : 128 * (k + 1)]
    parts[D:TAIL, :] = stats[...].astype(BF)
    for i in range(4):
        at = pl.multiple_of(40 * (4 * i + x), 8)
        tails[i] = jnp.concatenate([fresh[pl.ds(at, 40), :], jnp.zeros((8, 128), F32)], axis=0).astype(BF)
    ship(
        [(parts, far.at[i, pl.ds(0, TAIL)]) for i in range(4)]
        + [(tails.at[i], far.at[i, pl.ds(TAIL, BLOCK - TAIL)]) for i in range(4)],
        sems,
    )


def merge_shares(peaks, totals):
    peak = peaks[0]
    for p in peaks[1:]:
        peak = jnp.maximum(peak, p)
    shares = [jnp.exp(p - peak) for p in peaks]
    whole = shares[0] * totals[0]
    for share, total in zip(shares[1:], totals[1:]):
        whole = whole + share * total
    inverse = 1.0 / whole
    return [share * inverse for share in shares]


def tiles(rows):
    wide = jnp.concatenate([rows, jnp.zeros((8, 384 - FEATS), F32)], axis=1)
    return [wide[:, 128 * t : 128 * (t + 1)] for t in range(3)]


def rows_of(blocks, index):
    tail = blocks[index, FEATS:SEND, :].astype(F32)
    return [tail[0:8], tail[8:16], tail[16:24, :HEAD_DIM]]


def merge_kernel(
    place, parts_far, decodes, weight, hidden, hidden_dec, far, fresh_far, tall, out, fresh, parts, sems, land
):
    x = place[0] % 4
    lands = []
    for i in range(5):
        rows = pl.ds(FEATS * i, FEATS if i < 4 else BLOCK - D)
        lands.append(pltpu.make_async_copy(parts_far.at[:, rows], parts.at[:, rows], land.at[i]))
    for i in (4, 0, 1, 2, 3):
        lands[i].start()
    near = [decodes[s].astype(F32) for s in range(WID)]
    marks = [n[80:88] for n in near]
    shares = merge_shares(
        [m[:, 0:20] + m[:, 20:40] for m in marks], [m[:, 40:60] + m[:, 60:80] for m in marks]
    )
    low = iota((8, 128), 1) < HEAD_DIM
    decoded = [jnp.zeros((8, 128), F32) for t in range(10)]
    for s in range(WID):
        for t in range(10):
            share = jnp.where(low, shares[s][:, 2 * t : 2 * t + 1], shares[s][:, 2 * t + 1 : 2 * t + 2])
            decoded[t] = decoded[t] + share * near[s][8 * t : 8 * t + 8]
    rows = jnp.concatenate(decoded, axis=1).astype(BF)
    pick = (iota((8, DECODES), 1) == x // 2 * 8 + iota((8, DECODES), 0)).astype(BF)
    own_rows = dot(pick, hidden_dec[...], 1, 1) + dot(rows, weight[...], 1, 1)
    tail = jnp.concatenate(tiles(own_rows) + [jnp.zeros((8, 128), F32)], axis=0).astype(BF)
    lands[4].wait()
    extra = [parts[s, D:BLOCK, :].astype(F32) for s in range(4)]
    shares = merge_shares(
        [m[0:20] + m[20:40] for m in extra], [m[40:60] + m[60:80] for m in extra]
    )
    for s in range(4):
        fresh[:, 128 * s : 128 * (s + 1)] = extra[s][80:120]
    for h in range(HEADS):
        if h % 5 == 0:
            lands[h // 5].wait()
        rows = slice(HEAD_DIM * h, HEAD_DIM * (h + 1))
        total = shares[0][h : h + 1] * parts[0, rows, :].astype(F32)
        for s in range(1, 4):
            total = total + shares[s][h : h + 1] * parts[s, rows, :].astype(F32)
        tall[rows, :] = total.astype(BF)
    own = hidden[...].astype(F32) + dot(weight[...], tall[...], 1, 0)
    out[0:FEATS, :] = own.astype(BF)
    out[FEATS:SEND, :] = tail
    ship([(out, far.at[i]) for i in range(WID)] + [(fresh, fresh_far)], sems)


def ffn_kernel(place, far_weight, far_down, blocks, gain, far, residual, middle, weight, down, out, sems):
    w = place[0]
    weight_move = pltpu.make_async_copy(far_weight, weight, sems.at[0])
    down_move = pltpu.make_async_copy(far_down, down, sems.at[1])
    weight_move.start()
    down_move.start()
    for y in range(4):
        for x in range(4):
            middle[FEATS * y : FEATS * (y + 1), 128 * x : 128 * (x + 1)] = blocks[4 * y + x, 0:FEATS, :]
    rows = jnp.concatenate(
        [
            jnp.concatenate([t for y in range(4) for t in rows_of(blocks, 4 * y + x)], axis=1)
            for x in (0, 2)
        ],
        axis=0,
    )
    same = (iota((DECODES, DECODES), 0) == iota((DECODES, DECODES), 1)).astype(BF)
    middle[:, STRETCH:ROWS] = dot(rows.astype(BF), same, 0, 0).astype(BF)
    residual[...] = middle[pl.ds(pl.multiple_of(w * OWN, OWN), OWN), :]
    normed = norm_cols(middle[...], column(gain[...]))
    weight_move.wait()
    both = dot(weight[...], normed, 1, 0)
    gate, up = both[:FF_OWN], both[FF_OWN:]
    act = (gate / (1.0 + jnp.exp(-gate)) * up).astype(BF)
    down_move.wait()
    moves = []
    for i in range(4):
        part = dot(down[FEATS * i : FEATS * (i + 1), :], act, 1, 0).astype(BF)
        for j in range(4):
            out[4 * i + j] = part[OWN * j : OWN * (j + 1)]
        rows = pl.ds(4 * i, 4)
        moves.append(pltpu.make_async_copy(out.at[rows], far.at[rows], sems.at[2 + i]))
        moves[i].start()
    for move in moves:
        move.wait()


def final_kernel(parts, residual, out):
    total = residual[...].astype(F32)
    for s in range(WID):
        total = total + parts[s].astype(F32)
    out[...] = total.astype(BF)


VMEM = pl.BlockSpec(memory_space=pltpu.VMEM)
SMEM = pl.BlockSpec(memory_space=pltpu.SMEM)
ANY = pl.BlockSpec(memory_space=pltpu.HBM)


def call(kernel, outs, *args, scalars=0, anys=0, scratch=(), mib=16, far=False):
    many = isinstance(outs, list)
    count = len(outs) if many else 1
    kinds = [ANY if far is True or i < far else VMEM for i in range(count)]
    return pl.pallas_call(
        kernel,
        out_shape=outs,
        in_specs=[SMEM] * scalars + [ANY] * anys + [VMEM] * (len(args) - scalars - anys),
        out_specs=kinds if many else kinds[0],
        scratch_shapes=list(scratch),
        compiler_params=pltpu.CompilerParams(vmem_limit_bytes=int(mib * 1024 * 1024)),
        cost_estimate=pl.CostEstimate(flops=10**8, bytes_accessed=4 * 10**6, transcendentals=0),
    )(*args)


def shape(*dims, dtype=BF):
    return jax.ShapeDtypeStruct(dims, dtype)


def shards(hidden, w_qkv, w_out, w_gate, w_up, w_down, g_attn, g_ffn, lengths, k_cache, v_cache):
    y, x = lax.axis_index("y"), lax.axis_index("x")
    place = (4 * y + x).astype(jnp.int32).reshape(1)
    hidden_t = hidden.T

    def swap(blocks):
        return lax.all_to_all(blocks, ("y", "x"), 0, 0)

    k_tall, v_tall = k_cache.transpose(0, 2, 1), v_cache.transpose(0, 2, 1)
    all_hidden = swap(
        call(
            start_kernel,
            shape(WID, OWN, WIDE),
            hidden_t,
            k_tall,
            v_tall,
            anys=3,
            far=True,
            mib=62,
            scratch=(
                pltpu.VMEM((OWN, ROWS), BF),
                pltpu.VMEM((2 * KVW, 128), BF),
                pltpu.VMEM((WID, OWN, WIDE), BF),
                pltpu.SemaphoreType.DMA((3 + WID,)),
            ),
        )
    ).reshape(D, WIDE)
    first = lax.all_gather(
        lax.all_gather(
            call(first_kernel, shape(w_qkv.shape[0], 128), w_qkv), "core", axis=0, tiled=True
        ),
        "z",
        axis=0,
        tiled=True,
    )
    second = lax.all_gather(
        call(
            second_kernel,
            shape(w_gate.shape[0], 896),
            w_gate,
            w_up,
            w_down.T,
            w_out,
            anys=4,
            mib=62,
            scratch=(
                pltpu.VMEM(w_gate.shape, BF),
                pltpu.VMEM(w_up.shape, BF),
                pltpu.VMEM(w_down.shape[::-1], BF),
                pltpu.VMEM(w_out.shape, BF),
                pltpu.SemaphoreType.DMA((4,)),
            ),
        ),
        ("z", "core"),
        axis=0,
        tiled=True,
    )
    gate_up = jnp.concatenate([second[:, :FF_OWN], second[:, 256 : 256 + FF_OWN]], axis=1).T
    down = second[:, 512 : 512 + FF_OWN]
    sent = call(
        project_kernel,
        shape(WID, QKV_SEND, 128),
        place,
        all_hidden,
        first,
        g_attn.reshape(10, 128),
        scalars=1,
        far=True,
        scratch=(pltpu.VMEM((WID, QKV_SEND, 128), BF), pltpu.SemaphoreType.DMA((1,))),
    )
    mixed = swap(sent)
    places = jnp.concatenate([lengths[0] + jnp.arange(STRETCH), lengths[1:]]).astype(F32)
    ladder = jnp.arange(HALF).astype(F32) * (2.0 / HEAD_DIM)
    freqs = jnp.power(10000.0, -ladder)
    angles = freqs[:, None] * places[None, :STRETCH]
    flat = places[STRETCH:, None] * jnp.concatenate([freqs] * 4)[None, :]
    decodes, fresh_decode = call(
        decode_kernel,
        [shape(WID, 96, 128), shape(40, 128, dtype=F32)],
        lengths,
        place,
        k_tall,
        v_tall,
        mixed,
        jnp.concatenate([jnp.cos(flat), jnp.sin(flat)], axis=0),
        scalars=2,
        anys=2,
        far=True,
        mib=60,
        scratch=(
            pltpu.VMEM((2, 96, 128), BF),
            pltpu.VMEM((2 * KVW, 128), F32),
            pltpu.VMEM((GROUPS, 128, KVW), F32),
            pltpu.VMEM((GROUPS, 128, 128), F32),
            pltpu.VMEM((GROUPS, 128, KVW), F32),
            pltpu.VMEM((DECODES, KVW, SPAN), BF),
            pltpu.VMEM((DECODES, KVW, SPAN), BF),
            pltpu.SemaphoreType.DMA((2, WID + 1)),
        ),
    )
    decodes = swap(decodes)
    parts = call(
        prefill_kernel,
        shape(4, BLOCK, 128),
        lengths,
        place,
        mixed,
        jnp.cos(angles),
        jnp.sin(angles),
        scalars=2,
        far=True,
        mib=62,
        scratch=(
            pltpu.VMEM((WID * QKV_OWN, 128), F32),
            pltpu.VMEM((2 * KVW, 128), F32),
            pltpu.VMEM((KV_HEADS, KEYS, HEAD_DIM), BF),
            pltpu.VMEM((KVW, KEYS), BF),
            pltpu.VMEM((KEYS, 128), F32),
            pltpu.VMEM((4 * HEADS, 128), F32),
            pltpu.VMEM((TAIL, 128), BF),
            pltpu.VMEM((4, BLOCK - TAIL, 128), BF),
            pltpu.SemaphoreType.DMA((8,)),
        ),
    )
    own_hidden = lax.dynamic_slice(all_hidden, (FEATS * y, 128 * x), (FEATS, 128))
    own_decode = lax.dynamic_slice(all_hidden, (FEATS * y, STRETCH), (FEATS, DECODES))
    out_own = lax.all_gather(
        call(
            tall_kernel,
            shape(OWN, D),
            parts,
            second,
            anys=2,
            mib=61,
            scratch=(pltpu.VMEM((D, 128), BF), pltpu.SemaphoreType.DMA((1,))),
        ),
        "x",
        axis=0,
        tiled=True,
    )
    middle, fresh_own = call(
        merge_kernel,
        [shape(WID, SEND, 128), shape(40, STRETCH, dtype=F32)],
        place,
        lax.all_to_all(parts, "y", 0, 0),
        decodes,
        out_own,
        own_hidden,
        own_decode,
        scalars=1,
        anys=1,
        far=True,
        scratch=(
            pltpu.VMEM((D, 128), BF),
            pltpu.VMEM((SEND, 128), BF),
            pltpu.VMEM((40, STRETCH), F32),
            pltpu.VMEM((4, BLOCK, 128), BF),
            pltpu.SemaphoreType.DMA((WID + 1,)),
            pltpu.SemaphoreType.DMA((5,)),
        ),
    )
    new_kv = jnp.concatenate([fresh_own, fresh_decode[:, :DECODES]], axis=1).astype(BF).T
    sums, residual = call(
        ffn_kernel,
        [shape(WID, OWN, ROWS), shape(OWN, ROWS)],
        place,
        gate_up,
        down,
        swap(middle),
        g_ffn.reshape(10, 128),
        scalars=1,
        anys=2,
        far=1,
        mib=24,
        scratch=(
            pltpu.VMEM((D, ROWS), BF),
            pltpu.VMEM((2 * FF_OWN, D), BF),
            pltpu.VMEM((D, FF_OWN), BF),
            pltpu.VMEM((WID, OWN, ROWS), BF),
            pltpu.SemaphoreType.DMA((6,)),
        ),
    )
    output = call(final_kernel, shape(OWN, ROWS), swap(sums), residual)
    return (output.T, new_kv)


def solution(mesh):
    core = 2 if mesh.shape["tok"] % 2 == 0 else 1
    devices = mesh.devices.reshape(mesh.shape["tok"] // core, core, 4, 4)
    finer = jax.sharding.Mesh(devices, ("z", "core", "y", "x"))
    tok, wid = ("z", "core"), ("y", "x")
    placed = (
        P(tok, wid),
        P(tok, wid),
        P(tok, wid),
        P(tok, wid),
        P(tok, wid),
        P(wid, tok),
        P(),
        P(),
        P(tok),
        P(tok, wid, None),
        P(tok, wid, None),
    )
    return jax.shard_map(
        shards,
        mesh=finer,
        in_specs=placed,
        out_specs=(P(tok, wid), P(tok, wid)),
        check_vma=False,
    )
```

```python
import jax
import jax.numpy as jnp
from jax import lax
from jax.experimental import pallas as pl
from jax.experimental.pallas import tpu as pltpu
from jax.sharding import PartitionSpec as P

D = 1280
HEADS = 20
KV_HEADS = 5
GROUPS = 4
HEAD_DIM = 64
HALF = 32
STRETCH = 512
DECODES = 16
ROWS = 528
SPAN = 128
WID = 16
QKV_OWN = 120
OWN = 80
FF_OWN = 224
KVW = 320
OLD = 4 * SPAN
KEYS = OLD + STRETCH // 4
FEATS = 320
BLOCK = 1408
TAIL = 1360
SEND = 352
QKV_SEND = 304
WIDE = 640
PIECE = 40

EPSILON = 1e-05
MASKED = -(2.0**100)
SCALE = 0.125
BF = jnp.bfloat16
F32 = jnp.float32


def dot(a, b, ca, cb):
    return lax.dot_general(a, b, (((ca,), (cb,)), ((), ())), preferred_element_type=F32)


def iota(shape, axis):
    return lax.broadcasted_iota(jnp.int32, shape, axis)


def split(x):
    high = x.astype(BF)
    return high, (x - high.astype(F32)).astype(BF)


def column(gain):
    square = jnp.concatenate([gain, jnp.zeros((118, 128), F32)], axis=0).T
    return jnp.concatenate([square[:, i : i + 1] for i in range(10)], axis=0)


def norm_cols(tall, gain):
    wide = tall.astype(F32)
    mean_square = jnp.sum(wide * wide, axis=0, keepdims=True) * (1.0 / D)
    return (wide * lax.rsqrt(mean_square + EPSILON) * gain).astype(BF)


def ship(pairs, sems):
    moves = [pltpu.make_async_copy(a, b, sems.at[i]) for i, (a, b) in enumerate(pairs)]
    for move in moves:
        move.start()
    for move in moves:
        move.wait()


def start_kernel(
    hidden_far, k_far, v_far, gate_far, up_far, down_far, projection_far, far, packed,
    hidden, cache, out, gate, up, down, projection, sems, later
):
    late = [
        pltpu.make_async_copy(a, b, later.at[i])
        for i, (a, b) in enumerate(
            [(gate_far, gate), (up_far, up), (down_far, down), (projection_far, projection)]
        )
    ]
    ship(
        [
            (hidden_far, hidden),
            (k_far.at[0], cache.at[pl.ds(0, KVW)]),
            (v_far.at[0], cache.at[pl.ds(KVW, KVW)]),
        ],
        sems,
    )
    for move in late:
        move.start()
    main = hidden[:, 0:STRETCH]
    ending = hidden[:, STRETCH:ROWS].astype(F32)
    wide = cache[...].astype(F32)
    pad = jnp.zeros((OWN, 128 - DECODES - HEAD_DIM), F32)
    moves = []
    for i in range(WID):
        piece = wide[PIECE * i : PIECE * (i + 1)]
        halves = jnp.concatenate([piece[:, :HEAD_DIM], piece[:, HEAD_DIM:]], axis=0)
        out[i, :, 0:STRETCH] = main
        out[i, :, STRETCH:WIDE] = jnp.concatenate([ending, halves, pad], axis=1).astype(BF)
        moves.append(pltpu.make_async_copy(out.at[i], far.at[i], sems.at[3 + i]))
        moves[i].start()
    for move in late:
        move.wait()
    for i, ref in enumerate((gate, up, down)):
        packed[:, 256 * i : 256 * (i + 1)] = jnp.concatenate(
            [ref[...].astype(F32), jnp.zeros((packed.shape[0], 32), F32)], axis=1
        ).astype(BF)
    packed[:, 768:896] = jnp.concatenate(
        [projection[...].astype(F32), jnp.zeros((packed.shape[0], 48), F32)], axis=1
    ).astype(BF)
    for move in moves:
        move.wait()


def first_kernel(qkv, out):
    out[...] = jnp.concatenate(
        [qkv[...].astype(F32), jnp.zeros((out.shape[0], 8), F32)], axis=1
    ).astype(BF)


def tall_kernel(early, far, out, weight, sems):
    ship([(far.at[:, pl.ds(768, 128)], weight)], sems)
    out[...] = weight[...].astype(F32).T[:OWN].astype(BF)


def project_kernel(place, hidden, weight, gain, far, out, sems):
    w = place[0]
    normed = norm_cols(hidden[:, 0:ROWS], column(gain[...]))
    own = dot(weight[...], normed, 0, 0)
    same = (iota((128, 128), 0) == iota((128, 128), 1)).astype(BF)
    decoding = dot(own[:, STRETCH:ROWS].astype(BF), same, 0, 0).astype(BF)
    is_query = w * QKV_OWN + iota((128, 128), 0) < D
    for y in range(4):
        pieces = []
        for x in range(4):
            i = 4 * y + x
            ending = hidden[OWN * i : OWN * (i + 1), STRETCH:WIDE].astype(F32)
            ending = ending[:, DECODES : DECODES + HEAD_DIM]
            pieces.append(jnp.concatenate([ending[:PIECE], ending[PIECE:]], axis=1))
        caches = jnp.concatenate(pieces, axis=0).astype(BF)
        for x in range(4):
            block = jnp.where(
                is_query, own[:, 128 * x : 128 * (x + 1)], own[:, 128 * y : 128 * (y + 1)]
            )
            out[4 * y + x, 0:128, :] = block.astype(BF)
            out[4 * y + x, 128:144, :] = decoding
            out[4 * y + x, 144:QKV_SEND, :] = caches
    ship([(out, far)], sems)


def turn(x, cosine, sine):
    first, second = x[:HALF], x[HALF:]
    return jnp.concatenate(
        [first * cosine - second * sine, second * cosine + first * sine], axis=0
    )


def decode_kernel(lens, place, k_far, v_far, mixed, waves, far, fresh_far, out, fresh, qb, sc, od, k_cache, v_cache, sems):
    w = place[0]
    k_move = pltpu.make_async_copy(k_far.at[pl.ds(1, DECODES)], k_cache, sems.at[0, 0])
    v_move = pltpu.make_async_copy(v_far.at[pl.ds(1, DECODES)], v_cache, sems.at[0, 1])
    k_move.start()
    v_move.start()
    rows = jnp.concatenate(
        [mixed[i, 128:144, :].astype(F32)[:, :QKV_OWN] for i in range(WID)], axis=1
    )
    turned = rows[:, : D + KVW]
    ahead = pltpu.roll(turned, D + KVW - HALF, 1)
    behind = pltpu.roll(turned, HALF, 1)
    lane = iota((DECODES, D + KVW), 1) % HEAD_DIM
    cosine = jnp.concatenate([waves[0:DECODES, :]] * 13, axis=1)[:, : D + KVW]
    sine = jnp.concatenate([waves[DECODES : 2 * DECODES, :]] * 13, axis=1)[:, : D + KVW]
    turned = turned * cosine + jnp.where(lane < HALF, -ahead, behind) * sine
    turned = turned.astype(BF)
    both = jnp.concatenate([turned[:, D:].astype(F32), rows[:, D + KVW :]], axis=1).astype(BF)
    same = (iota((DECODES, 128), 0) == iota((DECODES, 128), 1)).astype(BF)
    fresh[...] = dot(both, same, 0, 0)
    pick = (iota((128, DECODES), 0) // 8 == iota((128, DECODES), 1)).astype(BF)
    place_g = (iota((8, KVW), 0) == iota((8, KVW), 1) // HEAD_DIM).astype(F32)
    grid_mask = jnp.broadcast_to(place_g[None], (DECODES, 8, KVW)).reshape(128, KVW)
    selves = dot(pick, both, 1, 0)
    k_self, v_self = selves[:, :KVW], selves[:, KVW:]
    own_row = iota((128, 1), 0) // 8 == w
    wide = turned.astype(F32)
    self_score = []
    for k in range(GROUPS):
        part = jnp.concatenate(
            [
                wide[:, HEAD_DIM * (GROUPS * g + k) : HEAD_DIM * (GROUPS * g + k + 1)]
                for g in range(KV_HEADS)
            ],
            axis=1,
        )
        query = dot(pick, part.astype(BF), 1, 0) * grid_mask * SCALE
        qb[k] = query
        self_score.append(
            jnp.where(own_row, jnp.sum(query * k_self, axis=1, keepdims=True), MASKED)
        )
    k_move.wait()
    for j in range(DECODES):
        query = jnp.concatenate([qb[k, 8 * j : 8 * j + 8, :] for k in range(GROUPS)], axis=0)
        score = dot(query.astype(BF), k_cache[j], 1, 0)
        spots = w * SPAN + iota((32, SPAN), 1)
        score = jnp.where(spots < lens[j + 1], score, MASKED)
        for k in range(GROUPS):
            sc[k, 8 * j : 8 * j + 8, :] = score[8 * k : 8 * k + 8]
    lane = iota((128, 128), 1)
    group = iota((128, 128), 0) % 8
    table = jnp.zeros((128, 128), F32)
    self_weight = []
    for k in range(GROUPS):
        head = jnp.where(group < KV_HEADS, GROUPS * group + k, 1000)
        score = sc[k]
        top, low = split(jnp.maximum(jnp.max(score, axis=1, keepdims=True), self_score[k]))
        top, low = top.astype(F32), low.astype(F32)
        expo = jnp.exp(score - (top + low))
        own = jnp.exp(self_score[k] - (top + low))
        total, rest = split(jnp.sum(expo, axis=1, keepdims=True) + own)
        sc[k] = expo
        self_weight.append(own)
        for i, part in enumerate((top, low, total.astype(F32), rest.astype(F32))):
            table = jnp.where(lane == HEADS * i + head, part, table)
    v_move.wait()
    for j in range(DECODES):
        expo = jnp.concatenate([sc[k, 8 * j : 8 * j + 8, :] for k in range(GROUPS)], axis=0)
        summed = dot(expo.astype(BF), v_cache[j], 1, 1)
        for k in range(GROUPS):
            od[k, 8 * j : 8 * j + 8, :] = summed[8 * k : 8 * k + 8]
    marks = dot(pick, table.astype(BF), 0, 0)
    flat = []
    for k in range(GROUPS):
        part = ((od[k] + self_weight[k] * v_self) * grid_mask).astype(BF)
        flat.append(dot(pick, part, 0, 0))
    decoded = jnp.concatenate(
        [flat[h % GROUPS][:, HEAD_DIM * (h // GROUPS) :][:, :HEAD_DIM] for h in range(HEADS)], axis=1
    )
    for half in range(2):
        rows = slice(8 * half, 8 * half + 8)
        block = jnp.concatenate(
            [decoded[rows, 128 * t : 128 * (t + 1)] for t in range(10)]
            + [marks[rows], jnp.zeros((8, 128), F32)],
            axis=0,
        ).astype(BF)
        out[half] = block
    at = pl.multiple_of(40 * w, 8)
    ship(
        [(out.at[i % 4 // 2], far.at[i]) for i in range(WID)] + [(fresh.at[pl.ds(at, 40)], fresh_far)],
        sems.at[1],
    )


def prefill_kernel(lens, place, mixed, cosine, sine, far, tall, fresh, keys, vals, bias, stats, parts, tails, sems):
    w = place[0]
    y, x = w // 4, w % 4
    for i in range(WID):
        tall[QKV_OWN * i : QKV_OWN * (i + 1), :] = mixed[i, 0:128, :].astype(F32)[:QKV_OWN]
    old = [mixed[i, 144:QKV_SEND, :].astype(F32) for i in range(WID)]
    caches = [
        jnp.concatenate([o[PIECE * i : PIECE * (i + 1)] for o in old], axis=0) for i in range(4)
    ]
    cols_x = pl.ds(pl.multiple_of(x * 128, 128), 128)
    cols_y = pl.ds(pl.multiple_of(y * 128, 128), 128)
    cos_x, sin_x, cos_y, sin_y = cosine[:, cols_x], sine[:, cols_x], cosine[:, cols_y], sine[:, cols_y]
    for g in range(KV_HEADS):
        rows = slice(HEAD_DIM * g, HEAD_DIM * (g + 1))
        turned = turn(tall[D + HEAD_DIM * g : D + HEAD_DIM * (g + 1), :], cos_y, sin_y).astype(BF)
        fresh[rows, :] = turned.astype(F32)
        keys[g, OLD:KEYS, :] = turned.astype(F32).T.astype(BF)
        for i in range(4):
            keys[g, 128 * i : 128 * (i + 1), :] = caches[i][rows].T.astype(BF)
    fresh[KVW:, :] = tall[D + KVW :, :]
    for i in range(4):
        vals[:, 128 * i : 128 * (i + 1)] = caches[i][KVW:].astype(BF)
    vals[:, OLD:KEYS] = tall[D + KVW :, :].astype(BF)
    spots = y * OLD + iota((OLD, 128), 0)
    bias[0:OLD, :] = jnp.where(spots < lens[0], 0.0, MASKED)
    later = x * 128 + iota((128, 128), 1)
    earlier = y * 128 + iota((128, 128), 0)
    bias[OLD:KEYS, :] = jnp.where(earlier <= later, 0.0, MASKED)
    for g in range(KV_HEADS):
        queries = []
        for k in range(GROUPS):
            at = HEAD_DIM * (GROUPS * g + k)
            query = turn(tall[at : at + HEAD_DIM, :], cos_x, sin_x)
            queries.append((query.astype(BF).astype(F32) * SCALE).astype(BF))
        scores = dot(keys[g], jnp.concatenate(queries, axis=1), 1, 0)
        expos = []
        for k in range(GROUPS):
            h = GROUPS * g + k
            score = scores[:, 128 * k : 128 * (k + 1)] + bias[...]
            top, low = split(jnp.max(score, axis=0, keepdims=True))
            top, low = top.astype(F32), low.astype(F32)
            expo = jnp.exp(score - (top + low))
            total, rest = split(jnp.sum(expo, axis=0, keepdims=True))
            for i, part in enumerate((top, low, total.astype(F32), rest.astype(F32))):
                stats[HEADS * i + h : HEADS * i + h + 1, :] = part
            expos.append(expo.astype(BF))
        summed = dot(
            vals[HEAD_DIM * g : HEAD_DIM * (g + 1), :], jnp.concatenate(expos, axis=1), 1, 0
        ).astype(BF)
        for k in range(GROUPS):
            h = GROUPS * g + k
            parts[HEAD_DIM * h : HEAD_DIM * (h + 1), :] = summed[:, 128 * k : 128 * (k + 1)]
    parts[D:TAIL, :] = stats[...].astype(BF)
    for i in range(4):
        at = pl.multiple_of(40 * (4 * i + x), 8)
        tails[i] = jnp.concatenate([fresh[pl.ds(at, 40), :], jnp.zeros((8, 128), F32)], axis=0).astype(BF)
    ship(
        [(parts, far.at[i, pl.ds(0, TAIL)]) for i in range(4)]
        + [(tails.at[i], far.at[i, pl.ds(TAIL, BLOCK - TAIL)]) for i in range(4)],
        sems,
    )


def merge_shares(peaks, totals):
    peak = peaks[0]
    for p in peaks[1:]:
        peak = jnp.maximum(peak, p)
    shares = [jnp.exp(p - peak) for p in peaks]
    whole = shares[0] * totals[0]
    for share, total in zip(shares[1:], totals[1:]):
        whole = whole + share * total
    inverse = 1.0 / whole
    return [share * inverse for share in shares]


def tiles(rows):
    wide = jnp.concatenate([rows, jnp.zeros((8, 384 - FEATS), F32)], axis=1)
    return [wide[:, 128 * t : 128 * (t + 1)] for t in range(3)]


def rows_of(blocks, index):
    tail = blocks[index, FEATS:SEND, :].astype(F32)
    return [tail[0:8], tail[8:16], tail[16:24, :HEAD_DIM]]


def merge_kernel(
    place, parts_far, decodes, weight, hidden, hidden_dec, far, fresh_far, tall, out, fresh, parts, sems, land
):
    x = place[0] % 4
    lands = []
    for i in range(5):
        rows = pl.ds(FEATS * i, FEATS if i < 4 else BLOCK - D)
        lands.append(pltpu.make_async_copy(parts_far.at[:, rows], parts.at[:, rows], land.at[i]))
    for i in (4, 0, 1, 2, 3):
        lands[i].start()
    near = [decodes[s].astype(F32) for s in range(WID)]
    marks = [n[80:88] for n in near]
    shares = merge_shares(
        [m[:, 0:20] + m[:, 20:40] for m in marks], [m[:, 40:60] + m[:, 60:80] for m in marks]
    )
    low = iota((8, 128), 1) < HEAD_DIM
    decoded = [jnp.zeros((8, 128), F32) for t in range(10)]
    for s in range(WID):
        for t in range(10):
            share = jnp.where(low, shares[s][:, 2 * t : 2 * t + 1], shares[s][:, 2 * t + 1 : 2 * t + 2])
            decoded[t] = decoded[t] + share * near[s][8 * t : 8 * t + 8]
    rows = jnp.concatenate(decoded, axis=1).astype(BF)
    pick = (iota((8, DECODES), 1) == x // 2 * 8 + iota((8, DECODES), 0)).astype(BF)
    own_rows = dot(pick, hidden_dec[...], 1, 1) + dot(rows, weight[...], 1, 1)
    tail = jnp.concatenate(tiles(own_rows) + [jnp.zeros((8, 128), F32)], axis=0).astype(BF)
    lands[4].wait()
    extra = [parts[s, D:BLOCK, :].astype(F32) for s in range(4)]
    shares = merge_shares(
        [m[0:20] + m[20:40] for m in extra], [m[40:60] + m[60:80] for m in extra]
    )
    for s in range(4):
        fresh[:, 128 * s : 128 * (s + 1)] = extra[s][80:120]
    for h in range(HEADS):
        if h % 5 == 0:
            lands[h // 5].wait()
        rows = slice(HEAD_DIM * h, HEAD_DIM * (h + 1))
        total = shares[0][h : h + 1] * parts[0, rows, :].astype(F32)
        for s in range(1, 4):
            total = total + shares[s][h : h + 1] * parts[s, rows, :].astype(F32)
        tall[rows, :] = total.astype(BF)
    own = hidden[...].astype(F32) + dot(weight[...], tall[...], 1, 0)
    out[0:FEATS, :] = own.astype(BF)
    out[FEATS:SEND, :] = tail
    ship([(out, far.at[i]) for i in range(WID)] + [(fresh, fresh_far)], sems)


def ffn_kernel(place, far_weight, far_down, blocks, gain, far, residual, middle, weight, down, out, sems):
    w = place[0]
    weight_move = pltpu.make_async_copy(far_weight, weight, sems.at[0])
    down_move = pltpu.make_async_copy(far_down, down, sems.at[1])
    weight_move.start()
    down_move.start()
    for y in range(4):
        for x in range(4):
            middle[FEATS * y : FEATS * (y + 1), 128 * x : 128 * (x + 1)] = blocks[4 * y + x, 0:FEATS, :]
    rows = jnp.concatenate(
        [
            jnp.concatenate([t for y in range(4) for t in rows_of(blocks, 4 * y + x)], axis=1)
            for x in (0, 2)
        ],
        axis=0,
    )
    same = (iota((DECODES, DECODES), 0) == iota((DECODES, DECODES), 1)).astype(BF)
    middle[:, STRETCH:ROWS] = dot(rows.astype(BF), same, 0, 0).astype(BF)
    residual[...] = middle[pl.ds(pl.multiple_of(w * OWN, OWN), OWN), :]
    normed = norm_cols(middle[...], column(gain[...]))
    weight_move.wait()
    both = dot(weight[...], normed, 1, 0)
    gate, up = both[:FF_OWN], both[FF_OWN:]
    act = (gate / (1.0 + jnp.exp(-gate)) * up).astype(BF)
    down_move.wait()
    moves = []
    for i in range(4):
        part = dot(down[FEATS * i : FEATS * (i + 1), :], act, 1, 0).astype(BF)
        for j in range(4):
            out[4 * i + j] = part[OWN * j : OWN * (j + 1)]
        rows = pl.ds(4 * i, 4)
        moves.append(pltpu.make_async_copy(out.at[rows], far.at[rows], sems.at[2 + i]))
        moves[i].start()
    for move in moves:
        move.wait()


def final_kernel(parts, residual, out):
    total = residual[...].astype(F32)
    for s in range(WID):
        total = total + parts[s].astype(F32)
    out[...] = total.astype(BF)


VMEM = pl.BlockSpec(memory_space=pltpu.VMEM)
SMEM = pl.BlockSpec(memory_space=pltpu.SMEM)
ANY = pl.BlockSpec(memory_space=pltpu.HBM)


def call(kernel, outs, *args, scalars=0, anys=0, scratch=(), mib=16, far=False):
    many = isinstance(outs, list)
    count = len(outs) if many else 1
    kinds = [ANY if far is True or i < far else VMEM for i in range(count)]
    return pl.pallas_call(
        kernel,
        out_shape=outs,
        in_specs=[SMEM] * scalars + [ANY] * anys + [VMEM] * (len(args) - scalars - anys),
        out_specs=kinds if many else kinds[0],
        scratch_shapes=list(scratch),
        compiler_params=pltpu.CompilerParams(vmem_limit_bytes=int(mib * 1024 * 1024)),
        cost_estimate=pl.CostEstimate(flops=10**8, bytes_accessed=4 * 10**6, transcendentals=0),
    )(*args)


def shape(*dims, dtype=BF):
    return jax.ShapeDtypeStruct(dims, dtype)


def shards(hidden, w_qkv, w_out, w_gate, w_up, w_down, g_attn, g_ffn, lengths, k_cache, v_cache):
    y, x = lax.axis_index("y"), lax.axis_index("x")
    place = (4 * y + x).astype(jnp.int32).reshape(1)
    hidden_t = hidden.T

    def swap(blocks):
        return lax.all_to_all(blocks, ("y", "x"), 0, 0)

    k_tall, v_tall = k_cache.transpose(0, 2, 1), v_cache.transpose(0, 2, 1)
    hidden_sent, packed = call(
        start_kernel,
        [shape(WID, OWN, WIDE), shape(w_gate.shape[0], 896)],
        hidden_t,
        k_tall,
        v_tall,
        w_gate,
        w_up,
        w_down.T,
        w_out,
        anys=7,
        far=1,
        mib=62,
        scratch=(
            pltpu.VMEM((OWN, ROWS), BF),
            pltpu.VMEM((2 * KVW, 128), BF),
            pltpu.VMEM((WID, OWN, WIDE), BF),
            pltpu.VMEM(w_gate.shape, BF),
            pltpu.VMEM(w_up.shape, BF),
            pltpu.VMEM(w_down.shape[::-1], BF),
            pltpu.VMEM(w_out.shape, BF),
            pltpu.SemaphoreType.DMA((3 + WID,)),
            pltpu.SemaphoreType.DMA((4,)),
        ),
    )
    all_hidden = swap(hidden_sent).reshape(D, WIDE)
    first = lax.all_gather(
        lax.all_gather(
            call(first_kernel, shape(w_qkv.shape[0], 128), w_qkv), "core", axis=0, tiled=True
        ),
        "z",
        axis=0,
        tiled=True,
    )
    second = lax.all_gather(
        packed,
        ("z", "core"),
        axis=0,
        tiled=True,
    )
    gate_up = jnp.concatenate([second[:, :FF_OWN], second[:, 256 : 256 + FF_OWN]], axis=1).T
    down = second[:, 512 : 512 + FF_OWN]
    sent = call(
        project_kernel,
        shape(WID, QKV_SEND, 128),
        place,
        all_hidden,
        first,
        g_attn.reshape(10, 128),
        scalars=1,
        far=True,
        scratch=(pltpu.VMEM((WID, QKV_SEND, 128), BF), pltpu.SemaphoreType.DMA((1,))),
    )
    mixed = swap(sent)
    places = jnp.concatenate([lengths[0] + jnp.arange(STRETCH), lengths[1:]]).astype(F32)
    ladder = jnp.arange(HALF).astype(F32) * (2.0 / HEAD_DIM)
    freqs = jnp.power(10000.0, -ladder)
    angles = freqs[:, None] * places[None, :STRETCH]
    flat = places[STRETCH:, None] * jnp.concatenate([freqs] * 4)[None, :]
    decodes, fresh_decode = call(
        decode_kernel,
        [shape(WID, 96, 128), shape(40, 128, dtype=F32)],
        lengths,
        place,
        k_tall,
        v_tall,
        mixed,
        jnp.concatenate([jnp.cos(flat), jnp.sin(flat)], axis=0),
        scalars=2,
        anys=2,
        far=True,
        mib=60,
        scratch=(
            pltpu.VMEM((2, 96, 128), BF),
            pltpu.VMEM((2 * KVW, 128), F32),
            pltpu.VMEM((GROUPS, 128, KVW), F32),
            pltpu.VMEM((GROUPS, 128, 128), F32),
            pltpu.VMEM((GROUPS, 128, KVW), F32),
            pltpu.VMEM((DECODES, KVW, SPAN), BF),
            pltpu.VMEM((DECODES, KVW, SPAN), BF),
            pltpu.SemaphoreType.DMA((2, WID + 1)),
        ),
    )
    decodes = swap(decodes)
    parts = call(
        prefill_kernel,
        shape(4, BLOCK, 128),
        lengths,
        place,
        mixed,
        jnp.cos(angles),
        jnp.sin(angles),
        scalars=2,
        far=True,
        mib=62,
        scratch=(
            pltpu.VMEM((WID * QKV_OWN, 128), F32),
            pltpu.VMEM((2 * KVW, 128), F32),
            pltpu.VMEM((KV_HEADS, KEYS, HEAD_DIM), BF),
            pltpu.VMEM((KVW, KEYS), BF),
            pltpu.VMEM((KEYS, 128), F32),
            pltpu.VMEM((4 * HEADS, 128), F32),
            pltpu.VMEM((TAIL, 128), BF),
            pltpu.VMEM((4, BLOCK - TAIL, 128), BF),
            pltpu.SemaphoreType.DMA((8,)),
        ),
    )
    own_hidden = lax.dynamic_slice(all_hidden, (FEATS * y, 128 * x), (FEATS, 128))
    own_decode = lax.dynamic_slice(all_hidden, (FEATS * y, STRETCH), (FEATS, DECODES))
    out_own = lax.all_gather(
        call(
            tall_kernel,
            shape(OWN, D),
            parts,
            second,
            anys=2,
            mib=61,
            scratch=(pltpu.VMEM((D, 128), BF), pltpu.SemaphoreType.DMA((1,))),
        ),
        "x",
        axis=0,
        tiled=True,
    )
    middle, fresh_own = call(
        merge_kernel,
        [shape(WID, SEND, 128), shape(40, STRETCH, dtype=F32)],
        place,
        lax.all_to_all(parts, "y", 0, 0),
        decodes,
        out_own,
        own_hidden,
        own_decode,
        scalars=1,
        anys=1,
        far=True,
        scratch=(
            pltpu.VMEM((D, 128), BF),
            pltpu.VMEM((SEND, 128), BF),
            pltpu.VMEM((40, STRETCH), F32),
            pltpu.VMEM((4, BLOCK, 128), BF),
            pltpu.SemaphoreType.DMA((WID + 1,)),
            pltpu.SemaphoreType.DMA((5,)),
        ),
    )
    new_kv = jnp.concatenate([fresh_own, fresh_decode[:, :DECODES]], axis=1).astype(BF).T
    sums, residual = call(
        ffn_kernel,
        [shape(WID, OWN, ROWS), shape(OWN, ROWS)],
        place,
        gate_up,
        down,
        swap(middle),
        g_ffn.reshape(10, 128),
        scalars=1,
        anys=2,
        far=1,
        mib=24,
        scratch=(
            pltpu.VMEM((D, ROWS), BF),
            pltpu.VMEM((2 * FF_OWN, D), BF),
            pltpu.VMEM((D, FF_OWN), BF),
            pltpu.VMEM((WID, OWN, ROWS), BF),
            pltpu.SemaphoreType.DMA((6,)),
        ),
    )
    output = call(final_kernel, shape(OWN, ROWS), swap(sums), residual)
    return (output.T, new_kv)


def solution(mesh):
    core = 2 if mesh.shape["tok"] % 2 == 0 else 1
    devices = mesh.devices.reshape(mesh.shape["tok"] // core, core, 4, 4)
    finer = jax.sharding.Mesh(devices, ("z", "core", "y", "x"))
    tok, wid = ("z", "core"), ("y", "x")
    placed = (
        P(tok, wid),
        P(tok, wid),
        P(tok, wid),
        P(tok, wid),
        P(tok, wid),
        P(wid, tok),
        P(),
        P(),
        P(tok),
        P(tok, wid, None),
        P(tok, wid, None),
    )
    return jax.shard_map(
        shards,
        mesh=finer,
        in_specs=placed,
        out_specs=(P(tok, wid), P(tok, wid)),
        check_vma=False,
    )
```
